32 devices in a mesh: dom: 4 (over z), grp: 8 (over y, x, core).
Axes of the slice: x: 2, y: 2, z: 4, core: 2. Of those that a mesh axis runs over, the one named last changes fastest.
Arguments:
- support: float32 [16, 16, 16, 4096], P(None, None, None, ('dom', 'grp')), may hold values from -6 to 6
- potential: float32 [16, 16, 16, 4096], P(None, None, None, ('dom', 'grp')), may hold values from -6 to 6
- magic_taps: float32 [16], replicated, may hold values from -1 to 1
- kinetic_taps: float32 [16], replicated, may hold values from -1 to 1
- kernel_diag: float32 [4096], P(('dom', 'grp')), may hold values from 0.2 to 5
- owners: int32 [4096, 1], P(('dom', 'grp')), may hold values from 0 to 7; in each aligned block of 128 rows (0 to 127, 128 to 255, ...) at most 24 rows name the same one
Outputs:
- margin: float32 [4096, 128], P(('dom', 'grp'))
- density: float32 [32, 256], P('dom')
The draws below stay inside these ranges and needn't reach their ends.
Inputs may be any that keep to these rules, and one draw needn't show every extreme that they name: `owners`: within each device's aligned block of 128 functions, no owner is named by more than 24 functions, a bound that some block reaches.
All inputs are finite; a program needn't handle non-finite values.
Results may differ from the reference program's by a relative error of at most 0.004.
Values may be sent and summed in bfloat16 or wider, within the bound.
A program may use at most 64 MiB of HBM per device.

```python
import math
import jax
import jax.numpy as jnp
import numpy as np
from jax import lax

BOX = 16
TAPS = 16
FDEV = 128
CAP = 24
NF = 4096
N_DOM = 4
N_GRP = 8


def levels(own_key, extent, cuts, smallest, high):
    loudness, own = 1.0, jax.random.fold_in(own_key, 6)
    for axis_at, blocks in cuts:
        steps = jnp.exp(jax.random.uniform(jax.random.fold_in(own, axis_at), (blocks,), jnp.float32, smallest / len(cuts), high / len(cuts)))
        loudness = loudness * jnp.repeat(steps, extent[axis_at] // blocks).reshape([-1 if axis == axis_at else 1 for axis in range(len(extent))])
    return loudness


def assign_block(own_key, own, number, rows, count, top, bound, slope):
    sequence = jax.random.permutation(own_key, count)
    packed, common = load_shares(count, rows * top, bound, slope, True), load_shares(count, rows * top, bound, slope, False)
    places = jnp.arange(count)

    def named(lengths, rotation):
        used = int((lengths > 0).sum())
        fixed = max(1, used // 4)
        moved = fixed + (places - fixed + rotation * (used - fixed)) % max(1, count - fixed)
        return jnp.zeros((count,), jnp.int32).at[sequence[jnp.where(places < fixed, places, moved)]].set(jnp.asarray(lengths, jnp.int32))

    lengths = jnp.where(number % 4 == 0, named(packed, number // 4), named(common, number - number // 4 - 1))
    mixed = jax.random.permutation(jax.random.fold_in(own, 3), count)
    donor, taker = mixed[0:count // 2 * 2:2], mixed[1:count // 2 * 2:2]
    room = jnp.minimum(lengths[donor] - 1, bound - lengths[taker]) // 2
    room = jnp.where((donor == sequence[0]) | (taker == sequence[0]) | (lengths[taker] == 0), 0, jnp.maximum(room, 0))
    moved = jax.random.randint(jax.random.fold_in(own, 4), (count // 2,), 0, 1 << 20) % (room + 1)
    lengths = lengths.at[donor].add(-moved).at[taker].add(moved)
    labels = jnp.searchsorted(jnp.cumsum(lengths), jnp.arange(rows * top), side="right").astype(jnp.int32)
    table = labels.reshape(top, rows).T
    table = table[jax.random.permutation(jax.random.fold_in(own, 1), rows)]
    rotation = jax.random.randint(jax.random.fold_in(own, 2), (rows, 1), 0, top)
    return jnp.take_along_axis(table, (jnp.arange(top)[None, :] + rotation) % top, axis=1)


def load_shares(number_of, total, bound, slope, full):
    portions = [(1 << 20) // math.isqrt(rank ** slope) + 1 for rank in range(1, number_of + 1)]
    largest = bound if full else min(bound, max(-(-total // number_of), total * portions[0] // sum(portions)))
    least = 1 if total - largest >= number_of - 1 else 0
    holding, spare = [largest] + [least] * (number_of - 1), total - largest - least * (number_of - 1)
    while spare > 0:
        movable = [i for i in range(1, number_of) if holding[i] < largest] or [i for i in range(1, number_of) if holding[i] < bound]
        mass, remaining = sum([portions[i] for i in movable]), spare
        for i in movable:
            extra = min(bound - holding[i], max(1, remaining * portions[i] // mass), spare)
            holding[i] = holding[i] + extra
            spare = spare - extra
    return np.array(holding)


def bell_draw(own_key, extent, spread, reach, shards=(), kind=jnp.bfloat16):
    entries = spread * jax.random.normal(own_key, extent, jnp.float32)
    if shards:
        entries = entries * levels(own_key, extent, shards, -0.22, 0.18)
    return jnp.clip(entries, -reach, reach).astype(kind)


def setup_inputs(seed: int = 0) -> dict:
    keys = jax.random.split(jax.random.key(seed), 7)
    support = bell_draw(keys[0], (BOX, BOX, BOX, NF), 1.0, 6.0, ((3, 32),), jnp.float32)
    potential = bell_draw(keys[1], (BOX, BOX, BOX, NF), 1.0, 6.0, ((3, 32),), jnp.float32)
    magic_taps = bell_draw(keys[2], (TAPS,), 0.25, 1.0, (), jnp.float32)
    kinetic_taps = bell_draw(keys[3], (TAPS,), 0.25, 1.0, (), jnp.float32)
    kernel_diag = jnp.clip(jnp.exp(math.log(5.0) - 3.218876 * jax.random.uniform(keys[4], (NF,), jnp.float32) ** levels(keys[4], (NF,), ((0, 32),), -0.2, 0.2)), 0.2, 5.0)
    owners_keys = jax.random.split(jax.random.fold_in(keys[5], 1), NF // FDEV)
    owners_turns = jax.random.permutation(jax.random.fold_in(keys[5], 3), NF // FDEV)
    owners = jax.vmap(lambda own, number: assign_block(jax.random.fold_in(keys[5], 2), own, number, FDEV, N_GRP, 1, CAP, 2))(owners_keys, owners_turns).reshape((NF, 1))
    return dict(support=support, potential=potential, magic_taps=magic_taps, kinetic_taps=kinetic_taps, kernel_diag=kernel_diag, owners=owners)


HIGHEST = lax.Precision.HIGHEST


def band_matrix(tap_values, box_side):
    row_index = jnp.arange(box_side)[:, None]
    col_index = jnp.arange(box_side)[None, :]
    offset = col_index - row_index + (tap_values.shape[0] // 2 - 1)
    tap_table = (offset[:, :, None] == jnp.arange(tap_values.shape[0])[None, None, :]).astype(jnp.float32)
    return jnp.einsum("abt,t->ab", tap_table, tap_values, precision=HIGHEST)


def filter_along(matrix, field_block, direction):
    if direction == 0:
        return jnp.einsum("ab,bjkf->ajkf", matrix, field_block, precision=HIGHEST)
    if direction == 1:
        return jnp.einsum("ab,ibkf->iakf", matrix, field_block, precision=HIGHEST)
    return jnp.einsum("ab,ijbf->ijaf", matrix, field_block, precision=HIGHEST)


def apply_block(support, potential, magic_taps, kinetic_taps, kernel_diag):
    box_side = support.shape[0]
    magic_band = band_matrix(magic_taps, box_side)
    kinetic_band = band_matrix(kinetic_taps, box_side)
    realspace = filter_along(magic_band, filter_along(magic_band, filter_along(magic_band, support, 0), 1), 2)
    density_part = jnp.sum(kernel_diag * realspace * realspace, axis=3)
    weighted = potential * realspace
    magic_back = magic_band.T
    returned = filter_along(magic_back, filter_along(magic_back, filter_along(magic_back, weighted, 0), 1), 2)
    kinetic_part = filter_along(kinetic_band, support, 0) + filter_along(kinetic_band, support, 1) + filter_along(kinetic_band, support, 2)
    gradient = (returned + kinetic_part).astype(jnp.bfloat16)
    return gradient, density_part


def reference(support, potential, magic_taps, kinetic_taps, kernel_diag, owners):
    box_side = support.shape[0]
    cell_count = box_side ** 3
    device_count = N_DOM * N_GRP
    scale_factor = 1.0 / float(box_side) ** 1.5

    def block(block_index):
        first_column = block_index * FDEV
        coeff_block = lax.dynamic_slice_in_dim(support, first_column, FDEV, 3)
        field_block = lax.dynamic_slice_in_dim(potential, first_column, FDEV, 3)
        kernel_block = lax.dynamic_slice_in_dim(kernel_diag, first_column, FDEV, 0)
        gradient, density_part = apply_block(coeff_block, field_block, magic_taps, kinetic_taps, kernel_block)
        return gradient.reshape(cell_count, FDEV), density_part / (FDEV * N_GRP)

    gradients, densities = lax.map(block, jnp.arange(device_count, dtype=jnp.int32))
    coeffs = support.reshape(cell_count, device_count, FDEV).astype(jnp.bfloat16)
    kernel_blocks = kernel_diag.reshape(device_count, FDEV)
    owner_blocks = owners.reshape(device_count, FDEV).astype(jnp.int32)

    def rows(block_index):
        domain = block_index // N_GRP
        target = (domain * N_GRP + owner_blocks[block_index]).astype(jnp.int32)
        operands = jnp.take(coeffs, target, axis=1).astype(jnp.float32)
        gradient = gradients[block_index].astype(jnp.float32)
        products = jnp.einsum("ci,cij->ij", gradient, operands, precision=HIGHEST)
        return products * jnp.take(kernel_blocks, target, axis=0) * scale_factor

    margin = lax.map(rows, jnp.arange(device_count, dtype=jnp.int32)).reshape(device_count * FDEV, FDEV)
    boxdens = jnp.sum(densities.reshape(N_DOM, N_GRP, box_side, box_side * box_side), axis=1)
    half_side = box_side // 2
    density = boxdens[:, :half_side] + jnp.roll(boxdens[:, half_side:], 1, axis=0)
    return margin, density.reshape(N_DOM * half_side, box_side * box_side)
```

```python
import functools

import jax
import jax.numpy as jnp
from jax import lax
from jax.experimental import pallas as pl
from jax.experimental.pallas import tpu as pltpu
from jax.sharding import PartitionSpec as P

HIGHEST = lax.Precision.HIGHEST


def passed_along(block, axis, distance):
    devices = range(lax.axis_size(axis))
    route = [((i - distance) % len(devices), i) for i in devices]
    return lax.ppermute(block, axis, route)


def band_matrix(tap_values, box_side):
    row_index = jnp.arange(box_side)[:, None]
    col_index = jnp.arange(box_side)[None, :]
    offset = col_index - row_index + (tap_values.shape[0] // 2 - 1)
    tap_table = (offset[:, :, None] == jnp.arange(tap_values.shape[0])[None, None, :]).astype(
        jnp.float32
    )
    return jnp.einsum("abt,t->ab", tap_table, tap_values, precision=HIGHEST)


def filter_along(matrix, field_block, direction):
    if direction == 0:
        return jnp.einsum("ab,bjkf->ajkf", matrix, field_block, precision=HIGHEST)
    if direction == 1:
        return jnp.einsum("ab,ibkf->iakf", matrix, field_block, precision=HIGHEST)
    return jnp.einsum("ab,ijbf->ijaf", matrix, field_block, precision=HIGHEST)


def apply_block(support, potential, magic_taps, kinetic_taps, kernel_diag):
    box_side = support.shape[0]
    magic_band = band_matrix(magic_taps, box_side)
    kinetic_band = band_matrix(kinetic_taps, box_side)
    realspace = filter_along(
        magic_band, filter_along(magic_band, filter_along(magic_band, support, 0), 1), 2
    )
    density_part = jnp.sum(kernel_diag * realspace * realspace, axis=3)
    weighted = potential * realspace
    magic_back = magic_band.T
    returned = filter_along(
        magic_back, filter_along(magic_back, filter_along(magic_back, weighted, 0), 1), 2
    )
    kinetic_part = (
        filter_along(kinetic_band, support, 0)
        + filter_along(kinetic_band, support, 1)
        + filter_along(kinetic_band, support, 2)
    )
    gradient = (returned + kinetic_part).astype(jnp.bfloat16)
    return (gradient, density_part)


def general_body(support, potential, magic_taps, kinetic_taps, kernel_diag, owners):
    box_side = support.shape[0]
    local_count = support.shape[3]
    cell_count = box_side**3
    half_side = box_side // 2
    groups = lax.axis_size("grp")
    capacity = max(2, 3 * local_count // (2 * groups))
    scale_factor = 1.0 / float(box_side) ** 1.5
    gradient, density_part = apply_block(support, potential, magic_taps, kinetic_taps, kernel_diag)
    density_part = (density_part / (local_count * groups)).reshape(box_side, box_side * box_side)
    target = owners[:, 0]
    onehot = (target[:, None] == jnp.arange(groups)[None, :]).astype(jnp.int32)
    before = jnp.cumsum(onehot, axis=0) - onehot
    slot_index = jnp.sum(before * onehot, axis=1)
    column = target * capacity + slot_index
    dispatch = (column[:, None] == jnp.arange(groups * capacity)[None, :]).astype(jnp.bfloat16)
    gradient_flat = gradient.reshape(cell_count, local_count)
    outgoing = lax.dot_general(
        dispatch, gradient_flat, (((0,), (1,)), ((), ())), preferred_element_type=jnp.float32
    ).astype(jnp.bfloat16)
    owned = support.reshape(cell_count, local_count).astype(jnp.bfloat16)
    received = lax.all_to_all(outgoing, "grp", split_axis=0, concat_axis=0, tiled=True)
    products = jnp.dot(received, owned, preferred_element_type=jnp.float32)
    products = products * (kernel_diag * scale_factor)[None, :]
    returned_rows = lax.all_to_all(products, "grp", split_axis=0, concat_axis=0, tiled=True)
    margin = jnp.dot(dispatch.astype(jnp.float32), returned_rows, precision=HIGHEST)
    summed = lax.psum(density_part, "grp")
    density_slab = summed[:half_side] + passed_along(summed[half_side:], "dom", 1)
    return (margin, density_slab)


MESH = pl.DeviceIdType.MESH
BF16 = jnp.bfloat16
F32 = jnp.float32
NT = (((1,), (1,)), ((), ()))


def split(value):
    high = value.astype(BF16)
    return high, (value - high.astype(F32)).astype(BF16)


def mm(left, right):
    return jnp.dot(left, right, preferred_element_type=F32)


def mm3(weight_high, weight_low, high, low):
    return mm(weight_high, high) + (mm(weight_high, low) + mm(weight_low, high))


def tap_select(offset, taps_ref):
    count = taps_ref.shape[0]
    value = jnp.zeros(offset.shape, F32)
    for tap in range(count):
        value = jnp.where(offset == tap - (count // 2 - 1), taps_ref[tap], value)
    return value


def fused_kernel(
    groups, doms, cap,
    magic_ref, kinetic_ref, owners_ref, kdiag_ref, support_ref, potential_ref,
    margin_ref, density_ref,
    x_ref, v_ref, y_ref, z_ref, xh_ref, xl_ref, w_ref, taps_ref, send_ref, recv_ref,
    acc_ref, dens_ref, halo_ref, comb_ref, prod_ref, back_ref, disp_ref, disp_t_ref,
    load_sem, send_sem, recv_sem, bs_sem, br_sem, ds_sem, dr_sem, hs_sem, hr_sem,
):
    side = x_ref.shape[0]
    funcs = x_ref.shape[3]
    plane = side * side
    chunks = side // 2
    slots = groups * cap
    me = lax.axis_index("grp")
    dom = lax.axis_index("dom")
    dom_next = lax.rem(dom + 1, doms)
    dom_prev = lax.rem(dom + doms - 1, doms)

    load_x = pltpu.make_async_copy(support_ref, x_ref, load_sem.at[0])
    load_v = pltpu.make_async_copy(potential_ref, v_ref, load_sem.at[1])
    load_x.start()
    load_v.start()

    barrier = pltpu.get_barrier_semaphore()
    for d in range(1, groups):
        pl.semaphore_signal(barrier, inc=1, device_id={"grp": lax.rem(me + d, groups)}, device_id_type=MESH)
    pl.semaphore_signal(barrier, inc=1, device_id={"dom": dom_prev}, device_id_type=MESH)

    for t in range(3 * side):
        taps_ref[t] = kinetic_ref[t - side] if side <= t < 2 * side else jnp.float32(0.0)
    row = lax.broadcasted_iota(jnp.int32, (side, plane), 0)
    col = lax.broadcasted_iota(jnp.int32, (side, plane), 1)
    outer = (col >> 4) - row
    inner = (col & 15) - row
    unit = jnp.where(outer == 0, 1.0, 0.0)
    tall = jnp.concatenate(
        [tap_select(outer, magic_ref), tap_select(-outer, magic_ref), tap_select(outer, kinetic_ref), unit],
        axis=1,
    )
    tall_high, tall_rest = split(tall)
    tall_mid = tall_rest
    tall_low = (tall - tall_high.astype(F32) - tall_mid.astype(F32)).astype(BF16)
    pick_row = lax.broadcasted_iota(jnp.int32, (plane, side), 0) >> 4
    pick_col = lax.broadcasted_iota(jnp.int32, (plane, side), 1)
    pick = jnp.where(pick_row == pick_col, 1.0, 0.0).astype(BF16)
    wide = mm(pick, tall_high) + (mm(pick, tall_mid) + mm(pick, tall_low))
    magic_out, back_out, kin_out, same_out = [wide[:, n * plane:(n + 1) * plane] for n in range(4)]

    def tiled(value):
        return jnp.concatenate([value] * side, axis=0)

    magic_in = tiled(tap_select(inner, magic_ref))
    back_in = tiled(tap_select(-inner, magic_ref))
    kin_in = tiled(tap_select(inner, kinetic_ref))
    same_in = tiled(jnp.where(inner == 0, 1.0, 0.0))
    matrices = [
        magic_out * magic_in,
        magic_out * same_in,
        back_out * back_in,
        back_out * same_in,
        kin_out * same_in + same_out * kin_in,
    ]
    for n, matrix in enumerate(matrices):
        high, low = split(matrix)
        w_ref[2 * n] = high
        w_ref[2 * n + 1] = low

    owner = owners_ref[...]
    named = jnp.where(lax.broadcasted_iota(jnp.int32, (16, funcs), 0) == owner, 1.0, 0.0)
    earlier = jnp.where(
        lax.broadcasted_iota(jnp.int32, (funcs, funcs), 0) < lax.broadcasted_iota(jnp.int32, (funcs, funcs), 1),
        1.0, 0.0,
    ).astype(BF16)
    before = mm(named.astype(BF16), earlier)
    slot = jnp.sum(before * named, axis=0, keepdims=True)
    column = owner.astype(F32) * float(cap) + slot
    padded = disp_t_ref.shape[1]
    spot = lax.broadcasted_iota(jnp.int32, (padded, funcs), 0).astype(F32)
    dispatch = jnp.where(spot == column, 1.0, 0.0)
    disp_ref[...] = dispatch[:slots].astype(BF16)
    disp_t_ref[...] = dispatch.T.astype(BF16)

    kdiag = kdiag_ref[...]
    kdiag_pair = jnp.concatenate([kdiag, kdiag], axis=1) * (1.0 / float(funcs * groups))
    dens_ref[...] = jnp.zeros_like(dens_ref)
    acc_ref[...] = jnp.zeros_like(acc_ref)

    def pair_mid(ref, n):
        first = ref[:, 2 * n].reshape(plane, funcs)
        second = ref[:, 2 * n + 1].reshape(plane, funcs)
        return jnp.concatenate([first, second], axis=1)

    def pair_top(ref, n):
        first = ref[2 * n].reshape(plane, funcs)
        second = ref[2 * n + 1].reshape(plane, funcs)
        return jnp.concatenate([first, second], axis=1)

    load_x.wait()

    def stage_a(n, carry):
        high, low = split(pair_mid(x_ref, n))
        xh_ref[n] = high
        xl_ref[n] = low
        out = mm3(w_ref[0], w_ref[1], high, low)
        y_ref[:, 2 * n] = out[:, :funcs].reshape(side, side, funcs)
        y_ref[:, 2 * n + 1] = out[:, funcs:].reshape(side, side, funcs)
        return carry

    lax.fori_loop(0, chunks, stage_a, 0)
    load_v.wait()

    dens_row = lax.broadcasted_iota(jnp.int32, (side, 2 * funcs), 0)
    dens_half = lax.broadcasted_iota(jnp.int32, (side, 2 * funcs), 1) >> 7

    def stage_b(n, carry):
        high, low = split(pair_top(y_ref, n))
        real = mm3(w_ref[2], w_ref[3], high, low)
        squared = (real * real * kdiag_pair).astype(BF16)
        chosen = jnp.where(dens_row == dens_half + 2 * n, 1.0, 0.0).astype(BF16)
        dens_ref[...] += lax.dot_general(chosen, squared, NT, preferred_element_type=F32)
        high, low = split(pair_top(v_ref, n) * real)
        out = mm3(w_ref[4], w_ref[5], high, low)
        z_ref[2 * n] = out[:, :funcs].reshape(side, side, funcs)
        z_ref[2 * n + 1] = out[:, funcs:].reshape(side, side, funcs)
        return carry

    lax.fori_loop(0, chunks, stage_b, 0)

    pl.semaphore_wait(barrier, groups)

    half = side // 2
    halo = pltpu.make_async_remote_copy(
        src_ref=dens_ref.at[pl.ds(half, half)], dst_ref=halo_ref, send_sem=hs_sem, recv_sem=hr_sem,
        device_id={"dom": dom_next}, device_id_type=MESH,
    )
    halo.start()

    order = [1 + (groups // 2 + n) % (groups - 1) for n in range(groups - 1)]

    def bulk(n, d):
        peer = lax.rem(me + d, groups)
        return pltpu.make_async_remote_copy(
            src_ref=send_ref.at[n, peer], dst_ref=recv_ref.at[n, me],
            send_sem=send_sem.at[n, d], recv_sem=recv_sem.at[n, d],
            device_id={"grp": peer}, device_id_type=MESH,
        )

    def arrived(n, d):
        source = lax.rem(me + groups - d, groups)
        return pltpu.make_async_remote_copy(
            src_ref=send_ref.at[n, source], dst_ref=recv_ref.at[n, source],
            send_sem=send_sem.at[n, d], recv_sem=recv_sem.at[n, d],
            device_id={"grp": source}, device_id_type=MESH,
        )

    def stage_c(n, carry):
        zh, zl = split(pair_mid(z_ref, n))
        grad = mm3(w_ref[6], w_ref[7], zh, zl) + mm3(w_ref[8], w_ref[9], xh_ref[n], xl_ref[n])
        rows = []
        for p in range(2):
            j = 2 * n + p
            along = jnp.zeros((side, side, funcs), F32)
            for other in range(side):
                along = along + taps_ref[other - j + (side // 2 - 1 + side)] * x_ref[:, other]
            block = (grad[:, p * funcs:(p + 1) * funcs] + along.reshape(plane, funcs)).astype(BF16)
            rows.append(lax.dot_general(disp_ref[...], block, NT, preferred_element_type=F32))
        for o in range(groups):
            send_ref[n, o] = jnp.concatenate(
                [rows[0][o * cap:(o + 1) * cap], rows[1][o * cap:(o + 1) * cap]], axis=0
            ).astype(BF16)
        for d in order:
            bulk(n, d).start()
        recv_ref[n, me] = send_ref[n, me]
        return carry

    lax.fori_loop(0, chunks // 2, stage_c, 0)

    halo.wait()
    comb_ref[me] = dens_ref[:half] + halo_ref[...]

    def spread(d, source):
        peer = lax.rem(me + d, groups)
        return pltpu.make_async_remote_copy(
            src_ref=comb_ref.at[source], dst_ref=comb_ref.at[source],
            send_sem=ds_sem.at[d], recv_sem=dr_sem.at[d],
            device_id={"grp": peer}, device_id_type=MESH,
        )

    for d in order:
        spread(d, me).start()

    lax.fori_loop(chunks // 2, chunks, stage_c, 0)

    def stage_d(n, carry):
        for d in order:
            arrived(n, d).wait_recv()
        rows = recv_ref[n].reshape(groups * 2 * cap, plane)
        acc_ref[...] += mm(rows, xh_ref[n])
        return carry

    lax.fori_loop(0, chunks, stage_d, 0)

    scale = kdiag * (1.0 / float(side) ** 1.5)
    for s in range(groups):
        top = 2 * cap * s
        prod_ref[s] = scale * (
            acc_ref[top:top + cap, :funcs] + acc_ref[top + cap:top + 2 * cap, funcs:]
        )

    def give(d):
        peer = lax.rem(me + d, groups)
        return pltpu.make_async_remote_copy(
            src_ref=prod_ref.at[peer], dst_ref=back_ref.at[me],
            send_sem=bs_sem.at[d], recv_sem=br_sem.at[d],
            device_id={"grp": peer}, device_id_type=MESH,
        )

    def get(d):
        source = lax.rem(me + groups - d, groups)
        return pltpu.make_async_remote_copy(
            src_ref=prod_ref.at[source], dst_ref=back_ref.at[source],
            send_sem=bs_sem.at[d], recv_sem=br_sem.at[d],
            device_id={"grp": source}, device_id_type=MESH,
        )

    for d in order:
        give(d).start()
    back_ref[me] = prod_ref[me]

    for d in order:
        spread(d, lax.rem(me + groups - d, groups)).wait_recv()
    total = comb_ref[0]
    for g in range(1, groups):
        total = total + comb_ref[g]
    density_ref[...] = total

    for d in order:
        get(d).wait_recv()
    returned = back_ref[...].reshape(slots, funcs)
    if padded > slots:
        returned = jnp.concatenate([returned, jnp.zeros((padded - slots, funcs), F32)], axis=0)
    high, low = split(returned)
    margin_ref[...] = mm(disp_t_ref[...], high) + mm(disp_t_ref[...], low)

    def drain(n, carry):
        for d in order:
            bulk(n, d).wait_send()
        return carry

    lax.fori_loop(0, chunks, drain, 0)
    for d in order:
        spread(d, me).wait_send()
        give(d).wait_send()


def fused_body(doms, support, potential, magic_taps, kinetic_taps, kernel_diag, owners):
    side = support.shape[0]
    funcs = support.shape[3]
    groups = lax.axis_size("grp")
    cap = max(2, 3 * funcs // (2 * groups))
    plane = side * side
    chunks = side // 2
    padded = -(-groups * cap // 128) * 128
    vmem = pl.BlockSpec(memory_space=pltpu.VMEM)
    smem = pl.BlockSpec(memory_space=pltpu.SMEM)
    anywhere = pl.BlockSpec(memory_space=pl.ANY)
    box = (side, side, side, funcs)
    dma = pltpu.SemaphoreType.DMA
    margin, density = pl.pallas_call(
        functools.partial(fused_kernel, groups, doms, cap),
        out_shape=(
            jax.ShapeDtypeStruct((funcs, funcs), F32),
            jax.ShapeDtypeStruct((side // 2, plane), F32),
        ),
        in_specs=[smem, smem, vmem, vmem, anywhere, anywhere],
        out_specs=(vmem, vmem),
        scratch_shapes=[
            pltpu.VMEM(box, F32),
            pltpu.VMEM(box, F32),
            pltpu.VMEM(box, F32),
            pltpu.VMEM(box, F32),
            pltpu.VMEM((chunks, plane, 2 * funcs), BF16),
            pltpu.VMEM((chunks, plane, 2 * funcs), BF16),
            pltpu.VMEM((10, plane, plane), BF16),
            pltpu.SMEM((3 * side,), F32),
            pltpu.VMEM((chunks, groups, 2 * cap, plane), BF16),
            pltpu.VMEM((chunks, groups, 2 * cap, plane), BF16),
            pltpu.VMEM((groups * 2 * cap, 2 * funcs), F32),
            pltpu.VMEM((side, plane), F32),
            pltpu.VMEM((side // 2, plane), F32),
            pltpu.VMEM((groups, side // 2, plane), F32),
            pltpu.VMEM((groups, cap, funcs), F32),
            pltpu.VMEM((groups, cap, funcs), F32),
            pltpu.VMEM((groups * cap, funcs), BF16),
            pltpu.VMEM((funcs, padded), BF16),
            dma((2,)),
            dma((chunks, groups)),
            dma((chunks, groups)),
            dma((groups,)),
            dma((groups,)),
            dma((groups,)),
            dma((groups,)),
            dma,
            dma,
        ],
        compiler_params=pltpu.CompilerParams(
            collective_id=0, has_side_effects=True, vmem_limit_bytes=40 * 2**20
        ),
    )(
        magic_taps, kinetic_taps, owners.reshape(1, funcs), kernel_diag.reshape(1, funcs),
        support, potential,
    )
    return (margin, density)


def body(doms, support, potential, magic_taps, kinetic_taps, kernel_diag, owners):
    side = support.shape[0]
    funcs = support.shape[3]
    groups = lax.axis_size("grp")
    cap = max(2, 3 * funcs // (2 * groups))
    fits = side == 16 and magic_taps.shape[0] == 16 and funcs == 128 and groups <= 8
    if fits and cap % 8 == 0 and doms > 1:
        return fused_body(doms, support, potential, magic_taps, kinetic_taps, kernel_diag, owners)
    return general_body(support, potential, magic_taps, kinetic_taps, kernel_diag, owners)


def solution(mesh):
    return jax.shard_map(
        functools.partial(body, mesh.shape["dom"]),
        mesh=mesh,
        in_specs=(
            P(None, None, None, ("dom", "grp")),
            P(None, None, None, ("dom", "grp")),
            P(),
            P(),
            P(("dom", "grp")),
            P(("dom", "grp"), None),
        ),
        out_specs=(P(("dom", "grp"), None), P("dom", None)),
        check_vma=False,
    )
```

```python
import functools

import jax
import jax.numpy as jnp
from jax import lax
from jax.experimental import pallas as pl
from jax.experimental.pallas import tpu as pltpu
from jax.sharding import PartitionSpec as P

HIGHEST = lax.Precision.HIGHEST


def passed_along(block, axis, distance):
    devices = range(lax.axis_size(axis))
    route = [((i - distance) % len(devices), i) for i in devices]
    return lax.ppermute(block, axis, route)


def band_matrix(tap_values, box_side):
    row_index = jnp.arange(box_side)[:, None]
    col_index = jnp.arange(box_side)[None, :]
    offset = col_index - row_index + (tap_values.shape[0] // 2 - 1)
    tap_table = (offset[:, :, None] == jnp.arange(tap_values.shape[0])[None, None, :]).astype(
        jnp.float32
    )
    return jnp.einsum("abt,t->ab", tap_table, tap_values, precision=HIGHEST)


def filter_along(matrix, field_block, direction):
    if direction == 0:
        return jnp.einsum("ab,bjkf->ajkf", matrix, field_block, precision=HIGHEST)
    if direction == 1:
        return jnp.einsum("ab,ibkf->iakf", matrix, field_block, precision=HIGHEST)
    return jnp.einsum("ab,ijbf->ijaf", matrix, field_block, precision=HIGHEST)


def apply_block(support, potential, magic_taps, kinetic_taps, kernel_diag):
    box_side = support.shape[0]
    magic_band = band_matrix(magic_taps, box_side)
    kinetic_band = band_matrix(kinetic_taps, box_side)
    realspace = filter_along(
        magic_band, filter_along(magic_band, filter_along(magic_band, support, 0), 1), 2
    )
    density_part = jnp.sum(kernel_diag * realspace * realspace, axis=3)
    weighted = potential * realspace
    magic_back = magic_band.T
    returned = filter_along(
        magic_back, filter_along(magic_back, filter_along(magic_back, weighted, 0), 1), 2
    )
    kinetic_part = (
        filter_along(kinetic_band, support, 0)
        + filter_along(kinetic_band, support, 1)
        + filter_along(kinetic_band, support, 2)
    )
    gradient = (returned + kinetic_part).astype(jnp.bfloat16)
    return (gradient, density_part)


def general_body(support, potential, magic_taps, kinetic_taps, kernel_diag, owners):
    box_side = support.shape[0]
    local_count = support.shape[3]
    cell_count = box_side**3
    half_side = box_side // 2
    groups = lax.axis_size("grp")
    capacity = max(2, 3 * local_count // (2 * groups))
    scale_factor = 1.0 / float(box_side) ** 1.5
    gradient, density_part = apply_block(support, potential, magic_taps, kinetic_taps, kernel_diag)
    density_part = (density_part / (local_count * groups)).reshape(box_side, box_side * box_side)
    target = owners[:, 0]
    onehot = (target[:, None] == jnp.arange(groups)[None, :]).astype(jnp.int32)
    before = jnp.cumsum(onehot, axis=0) - onehot
    slot_index = jnp.sum(before * onehot, axis=1)
    column = target * capacity + slot_index
    dispatch = (column[:, None] == jnp.arange(groups * capacity)[None, :]).astype(jnp.bfloat16)
    gradient_flat = gradient.reshape(cell_count, local_count)
    outgoing = lax.dot_general(
        dispatch, gradient_flat, (((0,), (1,)), ((), ())), preferred_element_type=jnp.float32
    ).astype(jnp.bfloat16)
    owned = support.reshape(cell_count, local_count).astype(jnp.bfloat16)
    received = lax.all_to_all(outgoing, "grp", split_axis=0, concat_axis=0, tiled=True)
    products = jnp.dot(received, owned, preferred_element_type=jnp.float32)
    products = products * (kernel_diag * scale_factor)[None, :]
    returned_rows = lax.all_to_all(products, "grp", split_axis=0, concat_axis=0, tiled=True)
    margin = jnp.dot(dispatch.astype(jnp.float32), returned_rows, precision=HIGHEST)
    summed = lax.psum(density_part, "grp")
    density_slab = summed[:half_side] + passed_along(summed[half_side:], "dom", 1)
    return (margin, density_slab)


MESH = pl.DeviceIdType.MESH
BF16 = jnp.bfloat16
F32 = jnp.float32
NT = (((1,), (1,)), ((), ()))


def split(value):
    high = value.astype(BF16)
    return high, (value - high.astype(F32)).astype(BF16)


def mm(left, right):
    return jnp.dot(left, right, preferred_element_type=F32)


def mm3(weight_high, weight_low, high, low):
    return mm(weight_high, high) + (mm(weight_high, low) + mm(weight_low, high))


def tap_select(offset, taps_ref):
    count = taps_ref.shape[0]
    value = jnp.zeros(offset.shape, F32)
    for tap in range(count):
        value = jnp.where(offset == tap - (count // 2 - 1), taps_ref[tap], value)
    return value


def fused_kernel(
    groups, doms, cap,
    magic_hbm, kinetic_hbm, owners_hbm, kdiag_hbm, support_ref, potential_ref,
    out_ref,
    magic_ref, kinetic_ref, owners_ref, kdiag_ref, x_ref, v_ref, y_ref, z_ref, xh_ref, xl_ref, w_ref, taps_ref, send_ref, recv_ref,
    acc_ref, dens_ref, halo_ref, comb_ref, prod_ref, back_ref, disp_ref, disp_t_ref,
    load_sem, send_sem, recv_sem, bs_sem, br_sem, ds_sem, dr_sem, hs_sem, hr_sem,
):
    side = x_ref.shape[0]
    funcs = x_ref.shape[3]
    plane = side * side
    chunks = side // 2
    slots = groups * cap
    me = lax.axis_index("grp")
    dom = lax.axis_index("dom")
    dom_next = lax.rem(dom + 1, doms)
    dom_prev = lax.rem(dom + doms - 1, doms)

    small = [
        pltpu.make_async_copy(magic_hbm, magic_ref, load_sem.at[0]),
        pltpu.make_async_copy(kinetic_hbm, kinetic_ref, load_sem.at[1]),
        pltpu.make_async_copy(owners_hbm, owners_ref, load_sem.at[2]),
        pltpu.make_async_copy(kdiag_hbm, kdiag_ref, load_sem.at[3]),
    ]
    part = side // 4
    load_x, load_v = [
        [
            pltpu.make_async_copy(
                source.at[pl.ds(part * n, part)], target.at[pl.ds(part * n, part)], load_sem.at[first + n]
            )
            for n in range(4)
        ]
        for source, target, first in ((support_ref, x_ref, 4), (potential_ref, v_ref, 8))
    ]
    for copy in small + load_x + load_v:
        copy.start()

    barrier = pltpu.get_barrier_semaphore()
    for d in range(1, groups):
        pl.semaphore_signal(barrier, inc=1, device_id={"grp": lax.rem(me + d, groups)}, device_id_type=MESH)
    pl.semaphore_signal(barrier, inc=1, device_id={"dom": dom_prev}, device_id_type=MESH)

    for copy in small:
        copy.wait()

    for t in range(3 * side):
        taps_ref[t] = kinetic_ref[t - side] if side <= t < 2 * side else jnp.float32(0.0)
    row = lax.broadcasted_iota(jnp.int32, (side, plane), 0)
    col = lax.broadcasted_iota(jnp.int32, (side, plane), 1)
    outer = (col >> 4) - row
    inner = (col & 15) - row
    unit = jnp.where(outer == 0, 1.0, 0.0)
    tall = jnp.concatenate(
        [tap_select(outer, magic_ref), tap_select(-outer, magic_ref), tap_select(outer, kinetic_ref), unit],
        axis=1,
    )
    tall_high, tall_rest = split(tall)
    tall_mid = tall_rest
    tall_low = (tall - tall_high.astype(F32) - tall_mid.astype(F32)).astype(BF16)
    pick_row = lax.broadcasted_iota(jnp.int32, (plane, side), 0) >> 4
    pick_col = lax.broadcasted_iota(jnp.int32, (plane, side), 1)
    pick = jnp.where(pick_row == pick_col, 1.0, 0.0).astype(BF16)
    wide = mm(pick, tall_high) + (mm(pick, tall_mid) + mm(pick, tall_low))
    magic_out, back_out, kin_out, same_out = [wide[:, n * plane:(n + 1) * plane] for n in range(4)]

    def tiled(value):
        return jnp.concatenate([value] * side, axis=0)

    magic_in = tiled(tap_select(inner, magic_ref))
    back_in = tiled(tap_select(-inner, magic_ref))
    kin_in = tiled(tap_select(inner, kinetic_ref))
    same_in = tiled(jnp.where(inner == 0, 1.0, 0.0))
    matrices = [
        magic_out * magic_in,
        magic_out * same_in,
        back_out * back_in,
        back_out * same_in,
        kin_out * same_in + same_out * kin_in,
    ]
    for n, matrix in enumerate(matrices):
        high, low = split(matrix)
        w_ref[2 * n] = high
        w_ref[2 * n + 1] = low

    owner = owners_ref[...]
    named = jnp.where(lax.broadcasted_iota(jnp.int32, (16, funcs), 0) == owner, 1.0, 0.0)
    earlier = jnp.where(
        lax.broadcasted_iota(jnp.int32, (funcs, funcs), 0) < lax.broadcasted_iota(jnp.int32, (funcs, funcs), 1),
        1.0, 0.0,
    ).astype(BF16)
    before = mm(named.astype(BF16), earlier)
    slot = jnp.sum(before * named, axis=0, keepdims=True)
    column = owner.astype(F32) * float(cap) + slot
    padded = disp_t_ref.shape[1]
    spot = lax.broadcasted_iota(jnp.int32, (padded, funcs), 0).astype(F32)
    dispatch = jnp.where(spot == column, 1.0, 0.0)
    disp_ref[...] = dispatch[:slots].astype(BF16)
    disp_t_ref[...] = dispatch.T.astype(BF16)

    kdiag = kdiag_ref[...]
    kdiag_pair = jnp.concatenate([kdiag, kdiag], axis=1) * (1.0 / float(funcs * groups))
    dens_ref[...] = jnp.zeros_like(dens_ref)
    acc_ref[...] = jnp.zeros_like(acc_ref)

    def pair_mid(ref, n):
        first = ref[:, 2 * n].reshape(plane, funcs)
        second = ref[:, 2 * n + 1].reshape(plane, funcs)
        return jnp.concatenate([first, second], axis=1)

    def pair_top(ref, n):
        first = ref[2 * n].reshape(plane, funcs)
        second = ref[2 * n + 1].reshape(plane, funcs)
        return jnp.concatenate([first, second], axis=1)

    for copy in load_x:
        copy.wait()

    def stage_a(n, carry):
        high, low = split(pair_mid(x_ref, n))
        xh_ref[n] = high
        xl_ref[n] = low
        out = mm3(w_ref[0], w_ref[1], high, low)
        y_ref[:, 2 * n] = out[:, :funcs].reshape(side, side, funcs)
        y_ref[:, 2 * n + 1] = out[:, funcs:].reshape(side, side, funcs)
        return carry

    for n in range(chunks):
        stage_a(n, 0)
    for copy in load_v:
        copy.wait()

    dens_row = lax.broadcasted_iota(jnp.int32, (side, 2 * funcs), 0)
    dens_half = lax.broadcasted_iota(jnp.int32, (side, 2 * funcs), 1) >> 7

    def stage_b(n, carry):
        high, low = split(pair_top(y_ref, n))
        real = mm3(w_ref[2], w_ref[3], high, low)
        squared = (real * real * kdiag_pair).astype(BF16)
        chosen = jnp.where(dens_row == dens_half + 2 * n, 1.0, 0.0).astype(BF16)
        dens_ref[...] += lax.dot_general(chosen, squared, NT, preferred_element_type=F32)
        high, low = split(pair_top(v_ref, n) * real)
        out = mm3(w_ref[4], w_ref[5], high, low)
        z_ref[2 * n] = out[:, :funcs].reshape(side, side, funcs)
        z_ref[2 * n + 1] = out[:, funcs:].reshape(side, side, funcs)
        return carry

    for n in range(chunks):
        stage_b(n, 0)

    pl.semaphore_wait(barrier, groups)

    half = side // 2
    halo = pltpu.make_async_remote_copy(
        src_ref=dens_ref.at[pl.ds(half, half)], dst_ref=halo_ref, send_sem=hs_sem, recv_sem=hr_sem,
        device_id={"dom": dom_next}, device_id_type=MESH,
    )
    halo.start()

    order = [1 + (groups // 2 + n) % (groups - 1) for n in range(groups - 1)]

    def bulk(n, d):
        peer = lax.rem(me + d, groups)
        return pltpu.make_async_remote_copy(
            src_ref=send_ref.at[n, peer], dst_ref=recv_ref.at[n, me],
            send_sem=send_sem.at[n, d], recv_sem=recv_sem.at[n, d],
            device_id={"grp": peer}, device_id_type=MESH,
        )

    def arrived(n, d):
        source = lax.rem(me + groups - d, groups)
        return pltpu.make_async_remote_copy(
            src_ref=send_ref.at[n, source], dst_ref=recv_ref.at[n, source],
            send_sem=send_sem.at[n, d], recv_sem=recv_sem.at[n, d],
            device_id={"grp": source}, device_id_type=MESH,
        )

    def stage_c(n, carry):
        zh, zl = split(pair_mid(z_ref, n))
        grad = mm3(w_ref[6], w_ref[7], zh, zl) + mm3(w_ref[8], w_ref[9], xh_ref[n], xl_ref[n])
        rows = []
        for p in range(2):
            j = 2 * n + p
            along = jnp.zeros((side, side, funcs), F32)
            for other in range(side):
                along = along + taps_ref[other - j + (side // 2 - 1 + side)] * x_ref[:, other]
            block = (grad[:, p * funcs:(p + 1) * funcs] + along.reshape(plane, funcs)).astype(BF16)
            rows.append(lax.dot_general(disp_ref[...], block, NT, preferred_element_type=F32))
        for o in range(groups):
            send_ref[n, o] = jnp.concatenate(
                [rows[0][o * cap:(o + 1) * cap], rows[1][o * cap:(o + 1) * cap]], axis=0
            ).astype(BF16)
        for d in order:
            bulk(n, d).start()
        recv_ref[n, me] = send_ref[n, me]
        return carry

    lax.fori_loop(0, chunks // 2, stage_c, 0)

    halo.wait()
    comb_ref[me] = dens_ref[:half] + halo_ref[...]

    def spread(d, source):
        peer = lax.rem(me + d, groups)
        return pltpu.make_async_remote_copy(
            src_ref=comb_ref.at[source], dst_ref=comb_ref.at[source],
            send_sem=ds_sem.at[d], recv_sem=dr_sem.at[d],
            device_id={"grp": peer}, device_id_type=MESH,
        )

    for d in order:
        spread(d, me).start()

    lax.fori_loop(chunks // 2, chunks, stage_c, 0)

    def stage_d(n, carry):
        for d in order:
            arrived(n, d).wait_recv()
        rows = recv_ref[n].reshape(groups * 2 * cap, plane)
        acc_ref[...] += mm(rows, xh_ref[n])
        return carry

    lax.fori_loop(0, chunks, stage_d, 0)

    scale = kdiag * (1.0 / float(side) ** 1.5)
    for s in range(groups):
        top = 2 * cap * s
        prod_ref[s] = scale * (
            acc_ref[top:top + cap, :funcs] + acc_ref[top + cap:top + 2 * cap, funcs:]
        )

    def give(d):
        peer = lax.rem(me + d, groups)
        return pltpu.make_async_remote_copy(
            src_ref=prod_ref.at[peer], dst_ref=back_ref.at[me],
            send_sem=bs_sem.at[d], recv_sem=br_sem.at[d],
            device_id={"grp": peer}, device_id_type=MESH,
        )

    def get(d):
        source = lax.rem(me + groups - d, groups)
        return pltpu.make_async_remote_copy(
            src_ref=prod_ref.at[source], dst_ref=back_ref.at[source],
            send_sem=bs_sem.at[d], recv_sem=br_sem.at[d],
            device_id={"grp": source}, device_id_type=MESH,
        )

    for d in order:
        give(d).start()
    back_ref[me] = prod_ref[me]

    for d in order:
        spread(d, lax.rem(me + groups - d, groups)).wait_recv()
    total = comb_ref[0]
    for g in range(1, groups):
        total = total + comb_ref[g]
    out_ref[:half] = total

    for d in order:
        get(d).wait_recv()
    returned = back_ref[...].reshape(slots, funcs)
    if padded > slots:
        returned = jnp.concatenate([returned, jnp.zeros((padded - slots, funcs), F32)], axis=0)
    high, low = split(returned)
    out_ref[half:, :funcs] = mm(disp_t_ref[...], high) + mm(disp_t_ref[...], low)
    out_ref[half:, funcs:] = jnp.zeros((funcs, plane - funcs), F32)

    def drain(n, carry):
        for d in order:
            bulk(n, d).wait_send()
        return carry

    lax.fori_loop(0, chunks, drain, 0)
    for d in order:
        spread(d, me).wait_send()
        give(d).wait_send()


def fused_body(doms, support, potential, magic_taps, kinetic_taps, kernel_diag, owners):
    side = support.shape[0]
    funcs = support.shape[3]
    groups = lax.axis_size("grp")
    cap = max(2, 3 * funcs // (2 * groups))
    plane = side * side
    chunks = side // 2
    padded = -(-groups * cap // 128) * 128
    vmem = pl.BlockSpec(memory_space=pltpu.VMEM)
    hbm = pl.BlockSpec(memory_space=pltpu.HBM)
    box = (side, side, side, funcs)
    dma = pltpu.SemaphoreType.DMA
    both = pl.pallas_call(
        functools.partial(fused_kernel, groups, doms, cap),
        out_shape=jax.ShapeDtypeStruct((side // 2 + funcs, plane), F32),
        in_specs=[hbm] * 6,
        out_specs=vmem,
        scratch_shapes=[
            pltpu.SMEM(magic_taps.shape, F32),
            pltpu.SMEM(kinetic_taps.shape, F32),
            pltpu.VMEM((1, funcs), jnp.int32),
            pltpu.VMEM((1, funcs), F32),
            pltpu.VMEM(box, F32),
            pltpu.VMEM(box, F32),
            pltpu.VMEM(box, F32),
            pltpu.VMEM(box, F32),
            pltpu.VMEM((chunks, plane, 2 * funcs), BF16),
            pltpu.VMEM((chunks, plane, 2 * funcs), BF16),
            pltpu.VMEM((10, plane, plane), BF16),
            pltpu.SMEM((3 * side,), F32),
            pltpu.VMEM((chunks, groups, 2 * cap, plane), BF16),
            pltpu.VMEM((chunks, groups, 2 * cap, plane), BF16),
            pltpu.VMEM((groups * 2 * cap, 2 * funcs), F32),
            pltpu.VMEM((side, plane), F32),
            pltpu.VMEM((side // 2, plane), F32),
            pltpu.VMEM((groups, side // 2, plane), F32),
            pltpu.VMEM((groups, cap, funcs), F32),
            pltpu.VMEM((groups, cap, funcs), F32),
            pltpu.VMEM((groups * cap, funcs), BF16),
            pltpu.VMEM((funcs, padded), BF16),
            dma((12,)),
            dma((chunks, groups)),
            dma((chunks, groups)),
            dma((groups,)),
            dma((groups,)),
            dma((groups,)),
            dma((groups,)),
            dma,
            dma,
        ],
        compiler_params=pltpu.CompilerParams(
            collective_id=0, has_side_effects=True, vmem_limit_bytes=63 * 2**20
        ),
    )(
        magic_taps, kinetic_taps, owners.reshape(1, funcs), kernel_diag.reshape(1, funcs),
        support, potential,
    )
    return (both[side // 2:, :funcs], both[:side // 2])


def body(doms, support, potential, magic_taps, kinetic_taps, kernel_diag, owners):
    side = support.shape[0]
    funcs = support.shape[3]
    groups = lax.axis_size("grp")
    cap = max(2, 3 * funcs // (2 * groups))
    fits = side == 16 and magic_taps.shape[0] == 16 and funcs == 128 and groups <= 8
    if fits and cap % 8 == 0 and doms > 1:
        return fused_body(doms, support, potential, magic_taps, kinetic_taps, kernel_diag, owners)
    return general_body(support, potential, magic_taps, kinetic_taps, kernel_diag, owners)


def solution(mesh):
    return jax.shard_map(
        functools.partial(body, mesh.shape["dom"]),
        mesh=mesh,
        in_specs=(
            P(None, None, None, ("dom", "grp")),
            P(None, None, None, ("dom", "grp")),
            P(),
            P(),
            P(("dom", "grp")),
            P(("dom", "grp"), None),
        ),
        out_specs=(P(("dom", "grp"), None), P("dom", None)),
        check_vma=False,
    )
```

```python
import functools

import jax
import jax.numpy as jnp
from jax import lax
from jax.experimental import pallas as pl
from jax.experimental.pallas import tpu as pltpu
from jax.sharding import PartitionSpec as P

HIGHEST = lax.Precision.HIGHEST


def passed_along(block, axis, distance):
    devices = range(lax.axis_size(axis))
    route = [((i - distance) % len(devices), i) for i in devices]
    return lax.ppermute(block, axis, route)


def band_matrix(tap_values, box_side):
    row_index = jnp.arange(box_side)[:, None]
    col_index = jnp.arange(box_side)[None, :]
    offset = col_index - row_index + (tap_values.shape[0] // 2 - 1)
    tap_table = (offset[:, :, None] == jnp.arange(tap_values.shape[0])[None, None, :]).astype(
        jnp.float32
    )
    return jnp.einsum("abt,t->ab", tap_table, tap_values, precision=HIGHEST)


def filter_along(matrix, field_block, direction):
    if direction == 0:
        return jnp.einsum("ab,bjkf->ajkf", matrix, field_block, precision=HIGHEST)
    if direction == 1:
        return jnp.einsum("ab,ibkf->iakf", matrix, field_block, precision=HIGHEST)
    return jnp.einsum("ab,ijbf->ijaf", matrix, field_block, precision=HIGHEST)


def apply_block(support, potential, magic_taps, kinetic_taps, kernel_diag):
    box_side = support.shape[0]
    magic_band = band_matrix(magic_taps, box_side)
    kinetic_band = band_matrix(kinetic_taps, box_side)
    realspace = filter_along(
        magic_band, filter_along(magic_band, filter_along(magic_band, support, 0), 1), 2
    )
    density_part = jnp.sum(kernel_diag * realspace * realspace, axis=3)
    weighted = potential * realspace
    magic_back = magic_band.T
    returned = filter_along(
        magic_back, filter_along(magic_back, filter_along(magic_back, weighted, 0), 1), 2
    )
    kinetic_part = (
        filter_along(kinetic_band, support, 0)
        + filter_along(kinetic_band, support, 1)
        + filter_along(kinetic_band, support, 2)
    )
    gradient = (returned + kinetic_part).astype(jnp.bfloat16)
    return (gradient, density_part)


def general_body(support, potential, magic_taps, kinetic_taps, kernel_diag, owners):
    box_side = support.shape[0]
    local_count = support.shape[3]
    cell_count = box_side**3
    half_side = box_side // 2
    groups = lax.axis_size("grp")
    capacity = max(2, 3 * local_count // (2 * groups))
    scale_factor = 1.0 / float(box_side) ** 1.5
    gradient, density_part = apply_block(support, potential, magic_taps, kinetic_taps, kernel_diag)
    density_part = (density_part / (local_count * groups)).reshape(box_side, box_side * box_side)
    target = owners[:, 0]
    onehot = (target[:, None] == jnp.arange(groups)[None, :]).astype(jnp.int32)
    before = jnp.cumsum(onehot, axis=0) - onehot
    slot_index = jnp.sum(before * onehot, axis=1)
    column = target * capacity + slot_index
    dispatch = (column[:, None] == jnp.arange(groups * capacity)[None, :]).astype(jnp.bfloat16)
    gradient_flat = gradient.reshape(cell_count, local_count)
    outgoing = lax.dot_general(
        dispatch, gradient_flat, (((0,), (1,)), ((), ())), preferred_element_type=jnp.float32
    ).astype(jnp.bfloat16)
    owned = support.reshape(cell_count, local_count).astype(jnp.bfloat16)
    received = lax.all_to_all(outgoing, "grp", split_axis=0, concat_axis=0, tiled=True)
    products = jnp.dot(received, owned, preferred_element_type=jnp.float32)
    products = products * (kernel_diag * scale_factor)[None, :]
    returned_rows = lax.all_to_all(products, "grp", split_axis=0, concat_axis=0, tiled=True)
    margin = jnp.dot(dispatch.astype(jnp.float32), returned_rows, precision=HIGHEST)
    summed = lax.psum(density_part, "grp")
    density_slab = summed[:half_side] + passed_along(summed[half_side:], "dom", 1)
    return (margin, density_slab)


MESH = pl.DeviceIdType.MESH
BF16 = jnp.bfloat16
F32 = jnp.float32
NT = (((1,), (1,)), ((), ()))


def split(value):
    high = value.astype(BF16)
    return high, (value - high.astype(F32)).astype(BF16)


def mm(left, right):
    return jnp.dot(left, right, preferred_element_type=F32)


def mm3(weight_high, weight_low, high, low):
    return mm(weight_high, high) + (mm(weight_high, low) + mm(weight_low, high))


def tap_select(offset, taps_ref):
    count = taps_ref.shape[0]
    value = jnp.zeros(offset.shape, F32)
    for tap in range(count):
        value = jnp.where(offset == tap - (count // 2 - 1), taps_ref[tap], value)
    return value


def fused_kernel(
    groups, doms, cap,
    magic_hbm, kinetic_hbm, owners_hbm, kdiag_hbm, support_ref, potential_ref,
    margin_ref, density_ref,
    magic_ref, kinetic_ref, owners_ref, kdiag_ref, x_ref, v_ref, y_ref, z_ref, xh_ref, xl_ref, w_ref, taps_ref, send_ref, recv_ref,
    acc_ref, dens_ref, halo_ref, comb_ref, prod_ref, back_ref, disp_ref, disp_t_ref,
    load_sem, send_sem, recv_sem, bs_sem, br_sem, ds_sem, dr_sem, hs_sem, hr_sem,
):
    side = x_ref.shape[0]
    funcs = x_ref.shape[3]
    plane = side * side
    chunks = side // 2
    slots = groups * cap
    me = lax.axis_index("grp")
    core = lax.rem(me, 2)
    dom = lax.axis_index("dom")
    dom_next = lax.rem(dom + 1, doms)
    dom_prev = lax.rem(dom + doms - 1, doms)

    small = [
        pltpu.make_async_copy(magic_hbm, magic_ref, load_sem.at[0]),
        pltpu.make_async_copy(kinetic_hbm, kinetic_ref, load_sem.at[1]),
        pltpu.make_async_copy(owners_hbm, owners_ref, load_sem.at[2]),
        pltpu.make_async_copy(kdiag_hbm, kdiag_ref, load_sem.at[3]),
    ]
    part = side // 4
    load_x, load_v = [
        [
            pltpu.make_async_copy(
                source.at[pl.ds(part * n, part)], target.at[pl.ds(part * n, part)], load_sem.at[first + n]
            )
            for n in range(4)
        ]
        for source, target, first in ((support_ref, x_ref, 4), (potential_ref, v_ref, 8))
    ]
    for copy in small + load_x + load_v:
        copy.start()

    barrier = pltpu.get_barrier_semaphore()
    for d in range(1, groups):
        pl.semaphore_signal(barrier, inc=1, device_id={"grp": lax.rem(me + d, groups)}, device_id_type=MESH)
    pl.semaphore_signal(barrier, inc=1, device_id={"dom": dom_prev}, device_id_type=MESH)

    for copy in small:
        copy.wait()

    for t in range(3 * side):
        taps_ref[t] = kinetic_ref[t - side] if side <= t < 2 * side else jnp.float32(0.0)
    row = lax.broadcasted_iota(jnp.int32, (side, plane), 0)
    col = lax.broadcasted_iota(jnp.int32, (side, plane), 1)
    outer = (col >> 4) - row
    inner = (col & 15) - row
    unit = jnp.where(outer == 0, 1.0, 0.0)
    tall = jnp.concatenate(
        [tap_select(outer, magic_ref), tap_select(-outer, magic_ref), tap_select(outer, kinetic_ref), unit],
        axis=1,
    )
    tall_high, tall_rest = split(tall)
    tall_mid = tall_rest
    tall_low = (tall - tall_high.astype(F32) - tall_mid.astype(F32)).astype(BF16)
    pick_row = lax.broadcasted_iota(jnp.int32, (plane, side), 0) >> 4
    pick_col = lax.broadcasted_iota(jnp.int32, (plane, side), 1)
    pick = jnp.where(pick_row == pick_col, 1.0, 0.0).astype(BF16)
    wide = mm(pick, tall_high) + (mm(pick, tall_mid) + mm(pick, tall_low))
    magic_out, back_out, kin_out, same_out = [wide[:, n * plane:(n + 1) * plane] for n in range(4)]

    def tiled(value):
        return jnp.concatenate([value] * side, axis=0)

    magic_in = tiled(tap_select(inner, magic_ref))
    back_in = tiled(tap_select(-inner, magic_ref))
    kin_in = tiled(tap_select(inner, kinetic_ref))
    same_in = tiled(jnp.where(inner == 0, 1.0, 0.0))
    matrices = [
        magic_out * magic_in,
        magic_out * same_in,
        back_out * back_in,
        back_out * same_in,
        kin_out * same_in + same_out * kin_in,
    ]

    def keep_matrix(n):
        high, low = split(matrices[n])
        w_ref[2 * n] = high
        w_ref[2 * n + 1] = low

    keep_matrix(0)

    kdiag = kdiag_ref[...]
    kdiag_pair = jnp.concatenate([kdiag, kdiag], axis=1) * (1.0 / float(funcs * groups))
    dens_ref[...] = jnp.zeros_like(dens_ref)
    acc_ref[...] = jnp.zeros_like(acc_ref)

    def pair_mid(ref, n):
        first = ref[:, 2 * n].reshape(plane, funcs)
        second = ref[:, 2 * n + 1].reshape(plane, funcs)
        return jnp.concatenate([first, second], axis=1)

    def pair_top(ref, n):
        first = ref[2 * n].reshape(plane, funcs)
        second = ref[2 * n + 1].reshape(plane, funcs)
        return jnp.concatenate([first, second], axis=1)

    for copy in load_x:
        copy.wait()

    def stage_a(n, carry):
        high, low = split(pair_mid(x_ref, n))
        xh_ref[n] = high
        xl_ref[n] = low
        out = mm3(w_ref[0], w_ref[1], high, low).astype(BF16)
        y_ref[:, 2 * n] = out[:, :funcs].reshape(side, side, funcs)
        y_ref[:, 2 * n + 1] = out[:, funcs:].reshape(side, side, funcs)
        return carry

    for n in range(chunks):
        stage_a(n, 0)
        if 1 <= n < 5:
            keep_matrix(n)

    owner = owners_ref[...]
    named = jnp.where(lax.broadcasted_iota(jnp.int32, (16, funcs), 0) == owner, 1.0, 0.0)
    earlier = jnp.where(
        lax.broadcasted_iota(jnp.int32, (funcs, funcs), 0) < lax.broadcasted_iota(jnp.int32, (funcs, funcs), 1),
        1.0, 0.0,
    ).astype(BF16)
    before = mm(named.astype(BF16), earlier)
    slot = jnp.sum(before * named, axis=0, keepdims=True)
    column = owner.astype(F32) * float(cap) + slot
    padded = disp_t_ref.shape[1]
    spot = lax.broadcasted_iota(jnp.int32, (padded, funcs), 0).astype(F32)
    dispatch = jnp.where(spot == column, 1.0, 0.0)
    disp_ref[...] = dispatch[:slots].astype(BF16)
    disp_t_ref[...] = dispatch.T.astype(BF16)

    for copy in load_v:
        copy.wait()

    dens_row = lax.broadcasted_iota(jnp.int32, (side, 2 * funcs), 0)
    dens_half = lax.broadcasted_iota(jnp.int32, (side, 2 * funcs), 1) >> 7

    def stage_b(n, carry):
        block = pair_top(y_ref, n)
        real = mm(w_ref[2], block) + mm(w_ref[3], block)
        squared = (real * real * kdiag_pair).astype(BF16)
        chosen = jnp.where(dens_row == dens_half + 2 * n, 1.0, 0.0).astype(BF16)
        dens_ref[...] += lax.dot_general(chosen, squared, NT, preferred_element_type=F32)
        block = (pair_top(v_ref, n) * real).astype(BF16)
        out = mm(w_ref[4], block) + mm(w_ref[5], block)
        z_ref[2 * n] = out[:, :funcs].reshape(side, side, funcs)
        z_ref[2 * n + 1] = out[:, funcs:].reshape(side, side, funcs)
        return carry

    for n in range(chunks):
        stage_b(n, 0)

    pl.semaphore_wait(barrier, groups)

    half = side // 2
    halo = pltpu.make_async_remote_copy(
        src_ref=dens_ref.at[pl.ds(half, half)], dst_ref=halo_ref, send_sem=hs_sem, recv_sem=hr_sem,
        device_id={"dom": dom_next}, device_id_type=MESH,
    )
    halo.start()

    order = range(1, groups)

    def partner(d):
        far, near = me // 4, lax.rem(me // 2, 2)
        return (
            lax.rem(far + d // 4, 2) * 4 + lax.rem(near + lax.rem(d // 2, 2), 2) * 2
            + lax.rem(core + lax.rem(d, 2), 2)
        )

    even, odd = (6, 2, 4, 7, 3, 5, 1), (4, 6, 2, 5, 7, 3, 1)
    sequence = [jnp.int32(a) + core * jnp.int32(b - a) for a, b in zip(even, odd)]

    def bulk(n, d):
        peer = partner(d)
        return pltpu.make_async_remote_copy(
            src_ref=send_ref.at[n, peer], dst_ref=recv_ref.at[n, me],
            send_sem=send_sem.at[n, d], recv_sem=recv_sem.at[n, d],
            device_id={"grp": peer}, device_id_type=MESH,
        )

    def arrived(n, d):
        source = partner(d)
        return pltpu.make_async_remote_copy(
            src_ref=send_ref.at[n, source], dst_ref=recv_ref.at[n, source],
            send_sem=send_sem.at[n, d], recv_sem=recv_sem.at[n, d],
            device_id={"grp": source}, device_id_type=MESH,
        )

    def stage_c(n, carry):
        zh, zl = split(pair_mid(z_ref, n))
        grad = mm3(w_ref[6], w_ref[7], zh, zl) + mm3(w_ref[8], w_ref[9], xh_ref[n], xl_ref[n])
        rows = []
        for p in range(2):
            j = 2 * n + p
            along = jnp.zeros((side, side, funcs), F32)
            for other in range(side):
                along = along + taps_ref[other - j + (side // 2 - 1 + side)] * x_ref[:, other]
            block = (grad[:, p * funcs:(p + 1) * funcs] + along.reshape(plane, funcs)).astype(BF16)
            rows.append(lax.dot_general(disp_ref[...], block, NT, preferred_element_type=F32))
        for o in range(groups):
            send_ref[n, o] = jnp.concatenate(
                [rows[0][o * cap:(o + 1) * cap], rows[1][o * cap:(o + 1) * cap]], axis=0
            ).astype(BF16)
        for d in sequence:
            bulk(n, d).start()
        recv_ref[n, me] = send_ref[n, me]
        return carry

    lax.fori_loop(0, chunks // 2, stage_c, 0)

    halo.wait()
    comb_ref[me] = dens_ref[:half] + halo_ref[...]

    def spread(d, source):
        peer = partner(d)
        return pltpu.make_async_remote_copy(
            src_ref=comb_ref.at[source], dst_ref=comb_ref.at[source],
            send_sem=ds_sem.at[d], recv_sem=dr_sem.at[d],
            device_id={"grp": peer}, device_id_type=MESH,
        )

    for d in sequence:
        spread(d, me).start()

    lax.fori_loop(chunks // 2, chunks, stage_c, 0)

    def stage_d(n, carry):
        for d in order:
            arrived(n, d).wait_recv()
        rows = recv_ref[n].reshape(groups * 2 * cap, plane)
        acc_ref[...] += mm(rows, xh_ref[n])
        return carry

    lax.fori_loop(0, chunks, stage_d, 0)

    scale = kdiag * (1.0 / float(side) ** 1.5)
    for s in range(groups):
        top = 2 * cap * s
        prod_ref[s] = scale * (
            acc_ref[top:top + cap, :funcs] + acc_ref[top + cap:top + 2 * cap, funcs:]
        )

    def give(d):
        peer = partner(d)
        return pltpu.make_async_remote_copy(
            src_ref=prod_ref.at[peer], dst_ref=back_ref.at[me],
            send_sem=bs_sem.at[d], recv_sem=br_sem.at[d],
            device_id={"grp": peer}, device_id_type=MESH,
        )

    def get(d):
        source = partner(d)
        return pltpu.make_async_remote_copy(
            src_ref=prod_ref.at[source], dst_ref=back_ref.at[source],
            send_sem=bs_sem.at[d], recv_sem=br_sem.at[d],
            device_id={"grp": source}, device_id_type=MESH,
        )

    for d in sequence:
        give(d).start()
    back_ref[me] = prod_ref[me]

    for d in order:
        spread(d, partner(d)).wait_recv()
    total = comb_ref[0]
    for g in range(1, groups):
        total = total + comb_ref[g]
    density_ref[...] = total

    for d in order:
        get(d).wait_recv()
    returned = back_ref[...].reshape(slots, funcs)
    if padded > slots:
        returned = jnp.concatenate([returned, jnp.zeros((padded - slots, funcs), F32)], axis=0)
    high, low = split(returned)
    margin_ref[...] = mm(disp_t_ref[...], high) + mm(disp_t_ref[...], low)

    def drain(n, carry):
        for d in order:
            bulk(n, d).wait_send()
        return carry

    lax.fori_loop(0, chunks, drain, 0)
    for d in order:
        spread(d, me).wait_send()
        give(d).wait_send()


def fused_body(doms, support, potential, magic_taps, kinetic_taps, kernel_diag, owners):
    side = support.shape[0]
    funcs = support.shape[3]
    groups = lax.axis_size("grp")
    cap = max(2, 3 * funcs // (2 * groups))
    plane = side * side
    chunks = side // 2
    padded = -(-groups * cap // 128) * 128
    vmem = pl.BlockSpec(memory_space=pltpu.VMEM)
    hbm = pl.BlockSpec(memory_space=pltpu.HBM)
    box = (side, side, side, funcs)
    dma = pltpu.SemaphoreType.DMA
    return pl.pallas_call(
        functools.partial(fused_kernel, groups, doms, cap),
        out_shape=(
            jax.ShapeDtypeStruct((funcs, funcs), F32),
            jax.ShapeDtypeStruct((side // 2, plane), F32),
        ),
        in_specs=[hbm] * 6,
        out_specs=(vmem, vmem),
        scratch_shapes=[
            pltpu.SMEM(magic_taps.shape, F32),
            pltpu.SMEM(kinetic_taps.shape, F32),
            pltpu.VMEM((1, funcs), jnp.int32),
            pltpu.VMEM((1, funcs), F32),
            pltpu.VMEM(box, F32),
            pltpu.VMEM(box, F32),
            pltpu.VMEM(box, BF16),
            pltpu.VMEM(box, F32),
            pltpu.VMEM((chunks, plane, 2 * funcs), BF16),
            pltpu.VMEM((chunks, plane, 2 * funcs), BF16),
            pltpu.VMEM((10, plane, plane), BF16),
            pltpu.SMEM((3 * side,), F32),
            pltpu.VMEM((chunks, groups, 2 * cap, plane), BF16),
            pltpu.VMEM((chunks, groups, 2 * cap, plane), BF16),
            pltpu.VMEM((groups * 2 * cap, 2 * funcs), F32),
            pltpu.VMEM((side, plane), F32),
            pltpu.VMEM((side // 2, plane), F32),
            pltpu.VMEM((groups, side // 2, plane), F32),
            pltpu.VMEM((groups, cap, funcs), F32),
            pltpu.VMEM((groups, cap, funcs), F32),
            pltpu.VMEM((groups * cap, funcs), BF16),
            pltpu.VMEM((funcs, padded), BF16),
            dma((12,)),
            dma((chunks, groups)),
            dma((chunks, groups)),
            dma((groups,)),
            dma((groups,)),
            dma((groups,)),
            dma((groups,)),
            dma,
            dma,
        ],
        compiler_params=pltpu.CompilerParams(
            collective_id=0, has_side_effects=True, vmem_limit_bytes=63 * 2**20
        ),
    )(
        magic_taps, kinetic_taps, owners.reshape(1, funcs), kernel_diag.reshape(1, funcs),
        support, potential,
    )


def body(doms, support, potential, magic_taps, kinetic_taps, kernel_diag, owners):
    side = support.shape[0]
    funcs = support.shape[3]
    groups = lax.axis_size("grp")
    cap = max(2, 3 * funcs // (2 * groups))
    fits = side == 16 and magic_taps.shape[0] == 16 and funcs == 128 and groups == 8
    if fits and cap % 8 == 0 and doms > 1:
        return fused_body(doms, support, potential, magic_taps, kinetic_taps, kernel_diag, owners)
    return general_body(support, potential, magic_taps, kinetic_taps, kernel_diag, owners)


def solution(mesh):
    return jax.shard_map(
        functools.partial(body, mesh.shape["dom"]),
        mesh=mesh,
        in_specs=(
            P(None, None, None, ("dom", "grp")),
            P(None, None, None, ("dom", "grp")),
            P(),
            P(),
            P(("dom", "grp")),
            P(("dom", "grp"), None),
        ),
        out_specs=(P(("dom", "grp"), None), P("dom", None)),
        check_vma=False,
    )
```

```python
import functools

import jax
import jax.numpy as jnp
from jax import lax
from jax.experimental import pallas as pl
from jax.experimental.pallas import tpu as pltpu
from jax.sharding import PartitionSpec as P

HIGHEST = lax.Precision.HIGHEST


def passed_along(block, axis, distance):
    devices = range(lax.axis_size(axis))
    route = [((i - distance) % len(devices), i) for i in devices]
    return lax.ppermute(block, axis, route)


def band_matrix(tap_values, box_side):
    row_index = jnp.arange(box_side)[:, None]
    col_index = jnp.arange(box_side)[None, :]
    offset = col_index - row_index + (tap_values.shape[0] // 2 - 1)
    tap_table = (offset[:, :, None] == jnp.arange(tap_values.shape[0])[None, None, :]).astype(
        jnp.float32
    )
    return jnp.einsum("abt,t->ab", tap_table, tap_values, precision=HIGHEST)


def filter_along(matrix, field_block, direction):
    if direction == 0:
        return jnp.einsum("ab,bjkf->ajkf", matrix, field_block, precision=HIGHEST)
    if direction == 1:
        return jnp.einsum("ab,ibkf->iakf", matrix, field_block, precision=HIGHEST)
    return jnp.einsum("ab,ijbf->ijaf", matrix, field_block, precision=HIGHEST)


def apply_block(support, potential, magic_taps, kinetic_taps, kernel_diag):
    box_side = support.shape[0]
    magic_band = band_matrix(magic_taps, box_side)
    kinetic_band = band_matrix(kinetic_taps, box_side)
    realspace = filter_along(
        magic_band, filter_along(magic_band, filter_along(magic_band, support, 0), 1), 2
    )
    density_part = jnp.sum(kernel_diag * realspace * realspace, axis=3)
    weighted = potential * realspace
    magic_back = magic_band.T
    returned = filter_along(
        magic_back, filter_along(magic_back, filter_along(magic_back, weighted, 0), 1), 2
    )
    kinetic_part = (
        filter_along(kinetic_band, support, 0)
        + filter_along(kinetic_band, support, 1)
        + filter_along(kinetic_band, support, 2)
    )
    gradient = (returned + kinetic_part).astype(jnp.bfloat16)
    return (gradient, density_part)


def general_body(support, potential, magic_taps, kinetic_taps, kernel_diag, owners):
    box_side = support.shape[0]
    local_count = support.shape[3]
    cell_count = box_side**3
    half_side = box_side // 2
    groups = lax.axis_size("grp")
    capacity = max(2, 3 * local_count // (2 * groups))
    scale_factor = 1.0 / float(box_side) ** 1.5
    gradient, density_part = apply_block(support, potential, magic_taps, kinetic_taps, kernel_diag)
    density_part = (density_part / (local_count * groups)).reshape(box_side, box_side * box_side)
    target = owners[:, 0]
    onehot = (target[:, None] == jnp.arange(groups)[None, :]).astype(jnp.int32)
    before = jnp.cumsum(onehot, axis=0) - onehot
    slot_index = jnp.sum(before * onehot, axis=1)
    column = target * capacity + slot_index
    dispatch = (column[:, None] == jnp.arange(groups * capacity)[None, :]).astype(jnp.bfloat16)
    gradient_flat = gradient.reshape(cell_count, local_count)
    outgoing = lax.dot_general(
        dispatch, gradient_flat, (((0,), (1,)), ((), ())), preferred_element_type=jnp.float32
    ).astype(jnp.bfloat16)
    owned = support.reshape(cell_count, local_count).astype(jnp.bfloat16)
    received = lax.all_to_all(outgoing, "grp", split_axis=0, concat_axis=0, tiled=True)
    products = jnp.dot(received, owned, preferred_element_type=jnp.float32)
    products = products * (kernel_diag * scale_factor)[None, :]
    returned_rows = lax.all_to_all(products, "grp", split_axis=0, concat_axis=0, tiled=True)
    margin = jnp.dot(dispatch.astype(jnp.float32), returned_rows, precision=HIGHEST)
    summed = lax.psum(density_part, "grp")
    density_slab = summed[:half_side] + passed_along(summed[half_side:], "dom", 1)
    return (margin, density_slab)


MESH = pl.DeviceIdType.MESH
BF16 = jnp.bfloat16
F32 = jnp.float32
NT = (((1,), (1,)), ((), ()))


def split(value):
    high = value.astype(BF16)
    return high, (value - high.astype(F32)).astype(BF16)


def mm(left, right):
    return jnp.dot(left, right, preferred_element_type=F32)


def mm3(weight_high, weight_low, high, low):
    return mm(weight_high, high) + (mm(weight_high, low) + mm(weight_low, high))


def tap_select(offset, taps_ref):
    count = taps_ref.shape[0]
    value = jnp.zeros(offset.shape, F32)
    for tap in range(count):
        value = jnp.where(offset == tap - (count // 2 - 1), taps_ref[tap], value)
    return value


def fused_kernel(
    groups, doms, cap,
    magic_hbm, kinetic_hbm, owners_hbm, kdiag_hbm, support_ref, potential_ref,
    margin_ref, density_ref,
    magic_ref, kinetic_ref, owners_ref, kdiag_ref, x_ref, v_ref, y_ref, z_ref, xh_ref, xl_ref, w_ref, taps_ref, send_ref, recv_ref,
    acc_ref, dens_ref, halo_ref, comb_ref, prod_ref, back_ref, disp_ref, disp_t_ref, cells_ref,
    load_sem, send_sem, recv_sem, bs_sem, br_sem, ds_sem, dr_sem, hs_sem, hr_sem,
):
    side = x_ref.shape[0]
    funcs = x_ref.shape[3]
    plane = side * side
    chunks = side // 2
    slots = groups * cap
    me = lax.axis_index("grp")
    core = lax.rem(me, 2)
    dom = lax.axis_index("dom")
    dom_next = lax.rem(dom + 1, doms)
    dom_prev = lax.rem(dom + doms - 1, doms)

    small = [
        pltpu.make_async_copy(magic_hbm, magic_ref, load_sem.at[0]),
        pltpu.make_async_copy(kinetic_hbm, kinetic_ref, load_sem.at[1]),
        pltpu.make_async_copy(owners_hbm, owners_ref, load_sem.at[2]),
        pltpu.make_async_copy(kdiag_hbm, kdiag_ref, load_sem.at[3]),
    ]
    part = side // 4
    load_x, load_v = [
        [
            pltpu.make_async_copy(
                source.at[pl.ds(part * n, part)], target.at[pl.ds(part * n, part)], load_sem.at[first + n]
            )
            for n in range(4)
        ]
        for source, target, first in ((support_ref, x_ref, 4), (potential_ref, v_ref, 8))
    ]
    for copy in small + load_x + load_v:
        copy.start()

    barrier = pltpu.get_barrier_semaphore()
    for d in range(1, groups):
        pl.semaphore_signal(barrier, inc=1, device_id={"grp": lax.rem(me + d, groups)}, device_id_type=MESH)
    pl.semaphore_signal(barrier, inc=1, device_id={"dom": dom_prev}, device_id_type=MESH)

    for copy in small:
        copy.wait()

    for t in range(3 * side):
        taps_ref[t] = kinetic_ref[t - side] if side <= t < 2 * side else jnp.float32(0.0)
    row = lax.broadcasted_iota(jnp.int32, (side, plane), 0)
    col = lax.broadcasted_iota(jnp.int32, (side, plane), 1)
    outer = (col >> 4) - row
    inner = (col & 15) - row
    unit = jnp.where(outer == 0, 1.0, 0.0)
    tall = jnp.concatenate(
        [tap_select(outer, magic_ref), tap_select(-outer, magic_ref), tap_select(outer, kinetic_ref), unit],
        axis=1,
    )
    tall_high, tall_rest = split(tall)
    tall_mid = tall_rest
    tall_low = (tall - tall_high.astype(F32) - tall_mid.astype(F32)).astype(BF16)
    pick_row = lax.broadcasted_iota(jnp.int32, (plane, side), 0) >> 4
    pick_col = lax.broadcasted_iota(jnp.int32, (plane, side), 1)
    pick = jnp.where(pick_row == pick_col, 1.0, 0.0).astype(BF16)
    wide = mm(pick, tall_high) + (mm(pick, tall_mid) + mm(pick, tall_low))
    magic_out, back_out, kin_out, same_out = [wide[:, n * plane:(n + 1) * plane] for n in range(4)]

    def tiled(value):
        return jnp.concatenate([value] * side, axis=0)

    magic_in = tiled(tap_select(inner, magic_ref))
    back_in = tiled(tap_select(-inner, magic_ref))
    kin_in = tiled(tap_select(inner, kinetic_ref))
    same_in = tiled(jnp.where(inner == 0, 1.0, 0.0))
    matrices = [
        magic_out * magic_in,
        magic_out * same_in,
        back_out * back_in,
        back_out * same_in,
        kin_out * same_in + same_out * kin_in,
    ]

    def keep_matrix(n):
        high, low = split(matrices[n])
        w_ref[2 * n] = high
        w_ref[2 * n + 1] = low

    keep_matrix(0)

    kdiag = kdiag_ref[...]
    kdiag_pair = jnp.concatenate([kdiag, kdiag], axis=1) * (1.0 / float(funcs * groups))
    cells_ref[...] = jnp.zeros_like(cells_ref)
    acc_ref[...] = jnp.zeros_like(acc_ref)

    def pair_mid(ref, n):
        first = ref[:, 2 * n].reshape(plane, funcs)
        second = ref[:, 2 * n + 1].reshape(plane, funcs)
        return jnp.concatenate([first, second], axis=1)

    def pair_top(ref, n):
        first = ref[2 * n].reshape(plane, funcs)
        second = ref[2 * n + 1].reshape(plane, funcs)
        return jnp.concatenate([first, second], axis=1)

    for copy in load_x:
        copy.wait()

    def stage_a(n, carry):
        high, low = split(pair_mid(x_ref, n))
        xh_ref[n] = high
        xl_ref[n] = low
        out = mm3(w_ref[0], w_ref[1], high, low).astype(BF16)
        y_ref[:, 2 * n] = out[:, :funcs].reshape(side, side, funcs)
        y_ref[:, 2 * n + 1] = out[:, funcs:].reshape(side, side, funcs)
        return carry

    for n in range(chunks):
        stage_a(n, 0)
        if 1 <= n < 5:
            keep_matrix(n)

    owner = owners_ref[...]
    named = jnp.where(lax.broadcasted_iota(jnp.int32, (16, funcs), 0) == owner, 1.0, 0.0)
    earlier = jnp.where(
        lax.broadcasted_iota(jnp.int32, (funcs, funcs), 0) < lax.broadcasted_iota(jnp.int32, (funcs, funcs), 1),
        1.0, 0.0,
    ).astype(BF16)
    before = mm(named.astype(BF16), earlier)
    slot = jnp.sum(before * named, axis=0, keepdims=True)
    column = owner.astype(F32) * float(cap) + slot
    padded = disp_t_ref.shape[1]
    spot = lax.broadcasted_iota(jnp.int32, (padded, funcs), 0).astype(F32)
    dispatch = jnp.where(spot == column, 1.0, 0.0)
    disp_ref[...] = dispatch[:slots].astype(BF16)
    disp_t_ref[...] = dispatch.T.astype(BF16)

    for copy in load_v:
        copy.wait()

    dens_lane = lax.broadcasted_iota(jnp.int32, (2 * funcs, funcs), 1)
    dens_half = lax.broadcasted_iota(jnp.int32, (2 * funcs, funcs), 0) >> 7

    def stage_b(n, carry):
        block = pair_top(y_ref, n)
        real = mm(w_ref[2], block) + mm(w_ref[3], block)
        squared = (real * real * kdiag_pair).astype(BF16)
        chosen = jnp.where(dens_lane == dens_half + 2 * n, 1.0, 0.0).astype(BF16)
        cells_ref[...] += mm(squared, chosen)
        block = (pair_top(v_ref, n) * real).astype(BF16)
        out = mm(w_ref[4], block) + mm(w_ref[5], block)
        z_ref[2 * n] = out[:, :funcs].reshape(side, side, funcs)
        z_ref[2 * n + 1] = out[:, funcs:].reshape(side, side, funcs)
        return carry

    for n in range(chunks):
        stage_b(n, 0)

    dens_ref[...] = cells_ref[...].T[:side]

    pl.semaphore_wait(barrier, groups)

    half = side // 2
    halo = pltpu.make_async_remote_copy(
        src_ref=dens_ref.at[pl.ds(half, half)], dst_ref=halo_ref, send_sem=hs_sem, recv_sem=hr_sem,
        device_id={"dom": dom_next}, device_id_type=MESH,
    )
    halo.start()

    order = range(1, groups)

    def partner(d):
        far, near = me // 4, lax.rem(me // 2, 2)
        return (
            lax.rem(far + d // 4, 2) * 4 + lax.rem(near + lax.rem(d // 2, 2), 2) * 2
            + lax.rem(core + lax.rem(d, 2), 2)
        )

    even, odd = (6, 2, 4, 7, 3, 5, 1), (4, 6, 2, 5, 7, 3, 1)
    sequence = [jnp.int32(a) + core * jnp.int32(b - a) for a, b in zip(even, odd)]

    def bulk(n, d):
        peer = partner(d)
        return pltpu.make_async_remote_copy(
            src_ref=send_ref.at[n, peer], dst_ref=recv_ref.at[n, me],
            send_sem=send_sem.at[n, d], recv_sem=recv_sem.at[n, d],
            device_id={"grp": peer}, device_id_type=MESH,
        )

    def arrived(n, d):
        source = partner(d)
        return pltpu.make_async_remote_copy(
            src_ref=send_ref.at[n, source], dst_ref=recv_ref.at[n, source],
            send_sem=send_sem.at[n, d], recv_sem=recv_sem.at[n, d],
            device_id={"grp": source}, device_id_type=MESH,
        )

    def chunk_rows(n):
        zh, zl = split(pair_mid(z_ref, n))
        grad = mm3(w_ref[6], w_ref[7], zh, zl) + mm3(w_ref[8], w_ref[9], xh_ref[n], xl_ref[n])
        rows = []
        for p in range(2):
            j = 2 * n + p
            along = jnp.zeros((side, side, funcs), F32)
            for other in range(side):
                along = along + taps_ref[other - j + (side // 2 - 1 + side)] * x_ref[:, other]
            block = (grad[:, p * funcs:(p + 1) * funcs] + along.reshape(plane, funcs)).astype(BF16)
            rows.append(lax.dot_general(disp_ref[...], block, NT, preferred_element_type=F32))
        return [
            jnp.concatenate(
                [rows[0][o * cap:(o + 1) * cap], rows[1][o * cap:(o + 1) * cap]], axis=0
            ).astype(BF16)
            for o in range(groups)
        ]

    def stage_c(numbers):
        made = [chunk_rows(n) for n in numbers]
        for n, blocks in zip(numbers, made):
            for o in range(groups):
                send_ref[n, o] = blocks[o]
        for n in numbers:
            for d in sequence:
                bulk(n, d).start()
        for n in numbers:
            recv_ref[n, me] = send_ref[n, me]

    def two_chunks(m, carry):
        stage_c((2 * m + 1, 2 * m + 2))
        return carry

    stage_c((0,))
    lax.fori_loop(0, chunks // 4, two_chunks, 0)

    halo.wait()
    comb_ref[me] = dens_ref[:half] + halo_ref[...]

    def spread(d, source):
        peer = partner(d)
        return pltpu.make_async_remote_copy(
            src_ref=comb_ref.at[source], dst_ref=comb_ref.at[source],
            send_sem=ds_sem.at[d], recv_sem=dr_sem.at[d],
            device_id={"grp": peer}, device_id_type=MESH,
        )

    for d in sequence:
        spread(d, me).start()

    lax.fori_loop(chunks // 4, chunks // 2 - 1, two_chunks, 0)
    stage_c((chunks - 1,))

    def stage_d(n, carry):
        for d in order:
            arrived(n, d).wait_recv()
        rows = recv_ref[n].reshape(groups * 2 * cap, plane)
        acc_ref[...] += mm(rows, xh_ref[n])
        return carry

    lax.fori_loop(0, chunks, stage_d, 0)

    scale = kdiag * (1.0 / float(side) ** 1.5)
    for s in range(groups):
        top = 2 * cap * s
        prod_ref[s] = scale * (
            acc_ref[top:top + cap, :funcs] + acc_ref[top + cap:top + 2 * cap, funcs:]
        )

    def give(d):
        peer = partner(d)
        return pltpu.make_async_remote_copy(
            src_ref=prod_ref.at[peer], dst_ref=back_ref.at[me],
            send_sem=bs_sem.at[d], recv_sem=br_sem.at[d],
            device_id={"grp": peer}, device_id_type=MESH,
        )

    def get(d):
        source = partner(d)
        return pltpu.make_async_remote_copy(
            src_ref=prod_ref.at[source], dst_ref=back_ref.at[source],
            send_sem=bs_sem.at[d], recv_sem=br_sem.at[d],
            device_id={"grp": source}, device_id_type=MESH,
        )

    for d in sequence:
        give(d).start()
    back_ref[me] = prod_ref[me]

    for d in order:
        spread(d, partner(d)).wait_recv()
    total = comb_ref[0]
    for g in range(1, groups):
        total = total + comb_ref[g]
    density_ref[...] = total

    for d in order:
        get(d).wait_recv()
    returned = back_ref[...].reshape(slots, funcs)
    if padded > slots:
        returned = jnp.concatenate([returned, jnp.zeros((padded - slots, funcs), F32)], axis=0)
    high, low = split(returned)
    margin_ref[...] = mm(disp_t_ref[...], high) + mm(disp_t_ref[...], low)

    def drain(n, carry):
        for d in order:
            bulk(n, d).wait_send()
        return carry

    lax.fori_loop(0, chunks, drain, 0)
    for d in order:
        spread(d, me).wait_send()
        give(d).wait_send()


def deliver_kernel(margin_ref, density_ref, margin_out, density_out, sem):
    copies = [
        pltpu.make_async_copy(margin_ref, margin_out, sem.at[0]),
        pltpu.make_async_copy(density_ref, density_out, sem.at[1]),
    ]
    for copy in copies:
        copy.start()
    for copy in copies:
        copy.wait()


def fused_body(doms, support, potential, magic_taps, kinetic_taps, kernel_diag, owners):
    side = support.shape[0]
    funcs = support.shape[3]
    groups = lax.axis_size("grp")
    cap = max(2, 3 * funcs // (2 * groups))
    plane = side * side
    chunks = side // 2
    padded = -(-groups * cap // 128) * 128
    vmem = pl.BlockSpec(memory_space=pltpu.VMEM)
    hbm = pl.BlockSpec(memory_space=pltpu.HBM)
    box = (side, side, side, funcs)
    dma = pltpu.SemaphoreType.DMA
    margin, density = pl.pallas_call(
        functools.partial(fused_kernel, groups, doms, cap),
        out_shape=(
            jax.ShapeDtypeStruct((funcs, funcs), F32),
            jax.ShapeDtypeStruct((side // 2, plane), F32),
        ),
        in_specs=[hbm] * 6,
        out_specs=(vmem, vmem),
        scratch_shapes=[
            pltpu.SMEM(magic_taps.shape, F32),
            pltpu.SMEM(kinetic_taps.shape, F32),
            pltpu.VMEM((1, funcs), jnp.int32),
            pltpu.VMEM((1, funcs), F32),
            pltpu.VMEM(box, F32),
            pltpu.VMEM(box, F32),
            pltpu.VMEM(box, BF16),
            pltpu.VMEM(box, F32),
            pltpu.VMEM((chunks, plane, 2 * funcs), BF16),
            pltpu.VMEM((chunks, plane, 2 * funcs), BF16),
            pltpu.VMEM((10, plane, plane), BF16),
            pltpu.SMEM((3 * side,), F32),
            pltpu.VMEM((chunks, groups, 2 * cap, plane), BF16),
            pltpu.VMEM((chunks, groups, 2 * cap, plane), BF16),
            pltpu.VMEM((groups * 2 * cap, 2 * funcs), F32),
            pltpu.VMEM((side, plane), F32),
            pltpu.VMEM((side // 2, plane), F32),
            pltpu.VMEM((groups, side // 2, plane), F32),
            pltpu.VMEM((groups, cap, funcs), F32),
            pltpu.VMEM((groups, cap, funcs), F32),
            pltpu.VMEM((groups * cap, funcs), BF16),
            pltpu.VMEM((funcs, padded), BF16),
            pltpu.VMEM((plane, funcs), F32),
            dma((12,)),
            dma((chunks, groups)),
            dma((chunks, groups)),
            dma((groups,)),
            dma((groups,)),
            dma((groups,)),
            dma((groups,)),
            dma,
            dma,
        ],
        compiler_params=pltpu.CompilerParams(
            collective_id=0, has_side_effects=True, vmem_limit_bytes=63 * 2**20
        ),
    )(
        magic_taps, kinetic_taps, owners.reshape(1, funcs), kernel_diag.reshape(1, funcs),
        support, potential,
    )
    return pl.pallas_call(
        deliver_kernel,
        out_shape=(
            jax.ShapeDtypeStruct(margin.shape, F32),
            jax.ShapeDtypeStruct(density.shape, F32),
        ),
        in_specs=[hbm, hbm],
        out_specs=(hbm, hbm),
        scratch_shapes=[dma((2,))],
        compiler_params=pltpu.CompilerParams(vmem_limit_bytes=63 * 2**20),
    )(margin, density)


def body(doms, support, potential, magic_taps, kinetic_taps, kernel_diag, owners):
    side = support.shape[0]
    funcs = support.shape[3]
    groups = lax.axis_size("grp")
    cap = max(2, 3 * funcs // (2 * groups))
    fits = side == 16 and magic_taps.shape[0] == 16 and funcs == 128 and groups == 8
    if fits and cap % 8 == 0 and doms > 1:
        return fused_body(doms, support, potential, magic_taps, kinetic_taps, kernel_diag, owners)
    return general_body(support, potential, magic_taps, kinetic_taps, kernel_diag, owners)


def solution(mesh):
    return jax.shard_map(
        functools.partial(body, mesh.shape["dom"]),
        mesh=mesh,
        in_specs=(
            P(None, None, None, ("dom", "grp")),
            P(None, None, None, ("dom", "grp")),
            P(),
            P(),
            P(("dom", "grp")),
            P(("dom", "grp"), None),
        ),
        out_specs=(P(("dom", "grp"), None), P("dom", None)),
        check_vma=False,
    )
```

```python
import functools

import jax
import jax.numpy as jnp
from jax import lax
from jax.experimental import pallas as pl
from jax.experimental.pallas import tpu as pltpu
from jax.sharding import PartitionSpec as P

HIGHEST = lax.Precision.HIGHEST


def passed_along(block, axis, distance):
    devices = range(lax.axis_size(axis))
    route = [((i - distance) % len(devices), i) for i in devices]
    return lax.ppermute(block, axis, route)


def band_matrix(tap_values, box_side):
    row_index = jnp.arange(box_side)[:, None]
    col_index = jnp.arange(box_side)[None, :]
    offset = col_index - row_index + (tap_values.shape[0] // 2 - 1)
    tap_table = (offset[:, :, None] == jnp.arange(tap_values.shape[0])[None, None, :]).astype(
        jnp.float32
    )
    return jnp.einsum("abt,t->ab", tap_table, tap_values, precision=HIGHEST)


def filter_along(matrix, field_block, direction):
    if direction == 0:
        return jnp.einsum("ab,bjkf->ajkf", matrix, field_block, precision=HIGHEST)
    if direction == 1:
        return jnp.einsum("ab,ibkf->iakf", matrix, field_block, precision=HIGHEST)
    return jnp.einsum("ab,ijbf->ijaf", matrix, field_block, precision=HIGHEST)


def apply_block(support, potential, magic_taps, kinetic_taps, kernel_diag):
    box_side = support.shape[0]
    magic_band = band_matrix(magic_taps, box_side)
    kinetic_band = band_matrix(kinetic_taps, box_side)
    realspace = filter_along(
        magic_band, filter_along(magic_band, filter_along(magic_band, support, 0), 1), 2
    )
    density_part = jnp.sum(kernel_diag * realspace * realspace, axis=3)
    weighted = potential * realspace
    magic_back = magic_band.T
    returned = filter_along(
        magic_back, filter_along(magic_back, filter_along(magic_back, weighted, 0), 1), 2
    )
    kinetic_part = (
        filter_along(kinetic_band, support, 0)
        + filter_along(kinetic_band, support, 1)
        + filter_along(kinetic_band, support, 2)
    )
    gradient = (returned + kinetic_part).astype(jnp.bfloat16)
    return (gradient, density_part)


def general_body(support, potential, magic_taps, kinetic_taps, kernel_diag, owners):
    box_side = support.shape[0]
    local_count = support.shape[3]
    cell_count = box_side**3
    half_side = box_side // 2
    groups = lax.axis_size("grp")
    capacity = max(2, 3 * local_count // (2 * groups))
    scale_factor = 1.0 / float(box_side) ** 1.5
    gradient, density_part = apply_block(support, potential, magic_taps, kinetic_taps, kernel_diag)
    density_part = (density_part / (local_count * groups)).reshape(box_side, box_side * box_side)
    target = owners[:, 0]
    onehot = (target[:, None] == jnp.arange(groups)[None, :]).astype(jnp.int32)
    before = jnp.cumsum(onehot, axis=0) - onehot
    slot_index = jnp.sum(before * onehot, axis=1)
    column = target * capacity + slot_index
    dispatch = (column[:, None] == jnp.arange(groups * capacity)[None, :]).astype(jnp.bfloat16)
    gradient_flat = gradient.reshape(cell_count, local_count)
    outgoing = lax.dot_general(
        dispatch, gradient_flat, (((0,), (1,)), ((), ())), preferred_element_type=jnp.float32
    ).astype(jnp.bfloat16)
    owned = support.reshape(cell_count, local_count).astype(jnp.bfloat16)
    received = lax.all_to_all(outgoing, "grp", split_axis=0, concat_axis=0, tiled=True)
    products = jnp.dot(received, owned, preferred_element_type=jnp.float32)
    products = products * (kernel_diag * scale_factor)[None, :]
    returned_rows = lax.all_to_all(products, "grp", split_axis=0, concat_axis=0, tiled=True)
    margin = jnp.dot(dispatch.astype(jnp.float32), returned_rows, precision=HIGHEST)
    summed = lax.psum(density_part, "grp")
    density_slab = summed[:half_side] + passed_along(summed[half_side:], "dom", 1)
    return (margin, density_slab)


MESH = pl.DeviceIdType.MESH
BF16 = jnp.bfloat16
F32 = jnp.float32
NT = (((1,), (1,)), ((), ()))


def split(value):
    high = value.astype(BF16)
    return high, (value - high.astype(F32)).astype(BF16)


def mm(left, right):
    return jnp.dot(left, right, preferred_element_type=F32)


def mm3(weight_high, weight_low, high, low):
    return mm(weight_high, high) + (mm(weight_high, low) + mm(weight_low, high))


def tap_select(offset, taps_ref):
    count = taps_ref.shape[0]
    value = jnp.zeros(offset.shape, F32)
    for tap in range(count):
        value = jnp.where(offset == tap - (count // 2 - 1), taps_ref[tap], value)
    return value


def fused_kernel(
    groups, doms, cap,
    magic_hbm, kinetic_hbm, owners_hbm, kdiag_hbm, support_ref, potential_ref,
    margin_ref, density_ref,
    magic_ref, kinetic_ref, owners_ref, kdiag_ref, x_ref, v_ref, y_ref, z_ref, xh_ref, xl_ref, w_ref, taps_ref, send_ref, recv_ref,
    acc_ref, dens_ref, halo_ref, comb_ref, prod_ref, back_ref, disp_ref, disp_t_ref, cells_ref,
    load_sem, send_sem, recv_sem, bs_sem, br_sem, ds_sem, dr_sem, hs_sem, hr_sem,
):
    side = x_ref.shape[0]
    funcs = x_ref.shape[3]
    plane = side * side
    chunks = side // 2
    slots = groups * cap
    me = lax.axis_index("grp")
    core = lax.rem(me, 2)
    dom = lax.axis_index("dom")
    dom_next = lax.rem(dom + 1, doms)
    dom_prev = lax.rem(dom + doms - 1, doms)

    small = [
        pltpu.make_async_copy(magic_hbm, magic_ref, load_sem.at[0]),
        pltpu.make_async_copy(kinetic_hbm, kinetic_ref, load_sem.at[1]),
        pltpu.make_async_copy(owners_hbm, owners_ref, load_sem.at[2]),
        pltpu.make_async_copy(kdiag_hbm, kdiag_ref, load_sem.at[3]),
    ]
    part = side // 4
    load_x, load_v = [
        [
            pltpu.make_async_copy(
                source.at[pl.ds(part * n, part)], target.at[pl.ds(part * n, part)], load_sem.at[first + n]
            )
            for n in range(4)
        ]
        for source, target, first in ((support_ref, x_ref, 4), (potential_ref, v_ref, 8))
    ]
    for copy in small + load_x + load_v:
        copy.start()

    barrier = pltpu.get_barrier_semaphore()
    for d in range(1, groups):
        pl.semaphore_signal(barrier, inc=1, device_id={"grp": lax.rem(me + d, groups)}, device_id_type=MESH)
    pl.semaphore_signal(barrier, inc=1, device_id={"dom": dom_prev}, device_id_type=MESH)

    for copy in small:
        copy.wait()

    for t in range(3 * side):
        taps_ref[t] = kinetic_ref[t - side] if side <= t < 2 * side else jnp.float32(0.0)
    row = lax.broadcasted_iota(jnp.int32, (side, plane), 0)
    col = lax.broadcasted_iota(jnp.int32, (side, plane), 1)
    outer = (col >> 4) - row
    inner = (col & 15) - row
    unit = jnp.where(outer == 0, 1.0, 0.0)
    tall = jnp.concatenate(
        [tap_select(outer, magic_ref), tap_select(-outer, magic_ref), tap_select(outer, kinetic_ref), unit],
        axis=1,
    )
    tall_high, tall_rest = split(tall)
    tall_mid = tall_rest
    tall_low = (tall - tall_high.astype(F32) - tall_mid.astype(F32)).astype(BF16)
    pick_row = lax.broadcasted_iota(jnp.int32, (plane, side), 0) >> 4
    pick_col = lax.broadcasted_iota(jnp.int32, (plane, side), 1)
    pick = jnp.where(pick_row == pick_col, 1.0, 0.0).astype(BF16)
    wide = mm(pick, tall_high) + (mm(pick, tall_mid) + mm(pick, tall_low))
    magic_out, back_out, kin_out, same_out = [wide[:, n * plane:(n + 1) * plane] for n in range(4)]

    def tiled(value):
        return jnp.concatenate([value] * side, axis=0)

    magic_in = tiled(tap_select(inner, magic_ref))
    back_in = tiled(tap_select(-inner, magic_ref))
    kin_in = tiled(tap_select(inner, kinetic_ref))
    same_in = tiled(jnp.where(inner == 0, 1.0, 0.0))
    matrices = [
        magic_out * magic_in,
        magic_out * same_in,
        back_out * back_in,
        back_out * same_in,
        kin_out * same_in + same_out * kin_in,
    ]

    def keep_matrix(n):
        high, low = split(matrices[n])
        w_ref[2 * n] = high
        w_ref[2 * n + 1] = low

    keep_matrix(0)

    kdiag = kdiag_ref[...]
    kdiag_pair = jnp.concatenate([kdiag, kdiag], axis=1) * (1.0 / float(funcs * groups))
    cells_ref[...] = jnp.zeros_like(cells_ref)
    acc_ref[...] = jnp.zeros_like(acc_ref)

    def pair_mid(ref, n):
        first = ref[:, 2 * n].reshape(plane, funcs)
        second = ref[:, 2 * n + 1].reshape(plane, funcs)
        return jnp.concatenate([first, second], axis=1)

    def pair_top(ref, n):
        first = ref[2 * n].reshape(plane, funcs)
        second = ref[2 * n + 1].reshape(plane, funcs)
        return jnp.concatenate([first, second], axis=1)

    for copy in load_x:
        copy.wait()

    def stage_a(n, carry):
        high, low = split(pair_mid(x_ref, n))
        xh_ref[n] = high
        xl_ref[n] = low
        out = mm3(w_ref[0], w_ref[1], high, low).astype(BF16)
        y_ref[:, 2 * n] = out[:, :funcs].reshape(side, side, funcs)
        y_ref[:, 2 * n + 1] = out[:, funcs:].reshape(side, side, funcs)
        return carry

    for n in range(chunks):
        stage_a(n, 0)
        if 1 <= n < 5:
            keep_matrix(n)

    owner = owners_ref[...]
    named = jnp.where(lax.broadcasted_iota(jnp.int32, (16, funcs), 0) == owner, 1.0, 0.0)
    earlier = jnp.where(
        lax.broadcasted_iota(jnp.int32, (funcs, funcs), 0) < lax.broadcasted_iota(jnp.int32, (funcs, funcs), 1),
        1.0, 0.0,
    ).astype(BF16)
    before = mm(named.astype(BF16), earlier)
    slot = jnp.sum(before * named, axis=0, keepdims=True)
    column = owner.astype(F32) * float(cap) + slot
    padded = disp_t_ref.shape[1]
    spot = lax.broadcasted_iota(jnp.int32, (padded, funcs), 0).astype(F32)
    dispatch = jnp.where(spot == column, 1.0, 0.0)
    disp_ref[...] = dispatch[:slots].astype(BF16)
    disp_t_ref[...] = dispatch.T.astype(BF16)

    for copy in load_v:
        copy.wait()

    dens_lane = lax.broadcasted_iota(jnp.int32, (2 * funcs, funcs), 1)
    dens_half = lax.broadcasted_iota(jnp.int32, (2 * funcs, funcs), 0) >> 7

    def stage_b(n, carry):
        block = pair_top(y_ref, n)
        real = mm(w_ref[2], block) + mm(w_ref[3], block)
        squared = (real * real * kdiag_pair).astype(BF16)
        chosen = jnp.where(dens_lane == dens_half + 2 * n, 1.0, 0.0).astype(BF16)
        cells_ref[...] += mm(squared, chosen)
        block = (pair_top(v_ref, n) * real).astype(BF16)
        out = mm(w_ref[4], block) + mm(w_ref[5], block)
        z_ref[2 * n] = out[:, :funcs].reshape(side, side, funcs)
        z_ref[2 * n + 1] = out[:, funcs:].reshape(side, side, funcs)
        return carry

    for n in range(chunks):
        stage_b(n, 0)

    dens_ref[...] = cells_ref[...].T[:side]

    pl.semaphore_wait(barrier, groups)

    half = side // 2
    halo = pltpu.make_async_remote_copy(
        src_ref=dens_ref.at[pl.ds(half, half)], dst_ref=halo_ref, send_sem=hs_sem, recv_sem=hr_sem,
        device_id={"dom": dom_next}, device_id_type=MESH,
    )
    halo.start()

    order = range(1, groups)

    def partner(d):
        far, near = me // 4, lax.rem(me // 2, 2)
        return (
            lax.rem(far + d // 4, 2) * 4 + lax.rem(near + lax.rem(d // 2, 2), 2) * 2
            + lax.rem(core + lax.rem(d, 2), 2)
        )

    even, odd = (6, 2, 4, 7, 3, 5, 1), (4, 6, 2, 5, 7, 3, 1)
    sequence = [jnp.int32(a) + core * jnp.int32(b - a) for a, b in zip(even, odd)]

    def bulk(n, d):
        peer = partner(d)
        return pltpu.make_async_remote_copy(
            src_ref=send_ref.at[n, peer], dst_ref=recv_ref.at[n, me],
            send_sem=send_sem.at[n, d], recv_sem=recv_sem.at[n, d],
            device_id={"grp": peer}, device_id_type=MESH,
        )

    def arrived(n, d):
        source = partner(d)
        return pltpu.make_async_remote_copy(
            src_ref=send_ref.at[n, source], dst_ref=recv_ref.at[n, source],
            send_sem=send_sem.at[n, d], recv_sem=recv_sem.at[n, d],
            device_id={"grp": source}, device_id_type=MESH,
        )

    def chunk_rows(n):
        zh, zl = split(pair_mid(z_ref, n))
        grad = mm3(w_ref[6], w_ref[7], zh, zl) + mm3(w_ref[8], w_ref[9], xh_ref[n], xl_ref[n])
        rows = []
        for p in range(2):
            j = 2 * n + p
            along = jnp.zeros((side, side, funcs), F32)
            for other in range(side):
                along = along + taps_ref[other - j + (side // 2 - 1 + side)] * x_ref[:, other]
            block = (grad[:, p * funcs:(p + 1) * funcs] + along.reshape(plane, funcs)).astype(BF16)
            rows.append(lax.dot_general(disp_ref[...], block, NT, preferred_element_type=F32))
        return [
            jnp.concatenate(
                [rows[0][o * cap:(o + 1) * cap], rows[1][o * cap:(o + 1) * cap]], axis=0
            ).astype(BF16)
            for o in range(groups)
        ]

    def stage_c(numbers):
        made = [chunk_rows(n) for n in numbers]
        for n, blocks in zip(numbers, made):
            for o in range(groups):
                send_ref[n, o] = blocks[o]
        for n in numbers:
            for d in sequence:
                bulk(n, d).start()
        for n in numbers:
            recv_ref[n, me] = send_ref[n, me]

    def two_chunks(m, carry):
        stage_c((2 * m + 1, 2 * m + 2))
        return carry

    stage_c((0,))
    lax.fori_loop(0, chunks // 4, two_chunks, 0)

    halo.wait()
    comb_ref[me] = dens_ref[:half] + halo_ref[...]

    def spread(d, source):
        peer = partner(d)
        return pltpu.make_async_remote_copy(
            src_ref=comb_ref.at[source], dst_ref=comb_ref.at[source],
            send_sem=ds_sem.at[d], recv_sem=dr_sem.at[d],
            device_id={"grp": peer}, device_id_type=MESH,
        )

    for d in sequence:
        spread(d, me).start()

    lax.fori_loop(chunks // 4, chunks // 2 - 1, two_chunks, 0)
    stage_c((chunks - 1,))

    def stage_d(n, carry):
        for d in order:
            arrived(n, d).wait_recv()
        rows = recv_ref[n].reshape(groups * 2 * cap, plane)
        acc_ref[...] += mm(rows, xh_ref[n])
        return carry

    lax.fori_loop(0, chunks, stage_d, 0)

    scale = kdiag * (1.0 / float(side) ** 1.5)
    for s in range(groups):
        top = 2 * cap * s
        prod_ref[s] = scale * (
            acc_ref[top:top + cap, :funcs] + acc_ref[top + cap:top + 2 * cap, funcs:]
        )

    def give(d):
        peer = partner(d)
        return pltpu.make_async_remote_copy(
            src_ref=prod_ref.at[peer], dst_ref=back_ref.at[me],
            send_sem=bs_sem.at[d], recv_sem=br_sem.at[d],
            device_id={"grp": peer}, device_id_type=MESH,
        )

    def get(d):
        source = partner(d)
        return pltpu.make_async_remote_copy(
            src_ref=prod_ref.at[source], dst_ref=back_ref.at[source],
            send_sem=bs_sem.at[d], recv_sem=br_sem.at[d],
            device_id={"grp": source}, device_id_type=MESH,
        )

    for d in sequence:
        give(d).start()
    back_ref[me] = prod_ref[me]

    for d in order:
        spread(d, partner(d)).wait_recv()
    total = comb_ref[0]
    for g in range(1, groups):
        total = total + comb_ref[g]
    density_ref[...] = total

    for d in order:
        get(d).wait_recv()
    returned = back_ref[...].reshape(slots, funcs)
    if padded > slots:
        returned = jnp.concatenate([returned, jnp.zeros((padded - slots, funcs), F32)], axis=0)
    high, low = split(returned)
    margin_ref[...] = mm(disp_t_ref[...], high) + mm(disp_t_ref[...], low)

    def drain(n, carry):
        for d in order:
            bulk(n, d).wait_send()
        return carry

    lax.fori_loop(0, chunks, drain, 0)
    for d in order:
        spread(d, me).wait_send()
        give(d).wait_send()


def fused_body(doms, support, potential, magic_taps, kinetic_taps, kernel_diag, owners):
    side = support.shape[0]
    funcs = support.shape[3]
    groups = lax.axis_size("grp")
    cap = max(2, 3 * funcs // (2 * groups))
    plane = side * side
    chunks = side // 2
    padded = -(-groups * cap // 128) * 128
    vmem = pl.BlockSpec(memory_space=pltpu.VMEM)
    hbm = pl.BlockSpec(memory_space=pltpu.HBM)
    box = (side, side, side, funcs)
    dma = pltpu.SemaphoreType.DMA
    margin, density = pl.pallas_call(
        functools.partial(fused_kernel, groups, doms, cap),
        out_shape=(
            pltpu.VMEM((funcs, funcs), F32),
            pltpu.VMEM((side // 2, plane), F32),
        ),
        in_specs=[hbm] * 6,
        out_specs=(vmem, vmem),
        scratch_shapes=[
            pltpu.SMEM(magic_taps.shape, F32),
            pltpu.SMEM(kinetic_taps.shape, F32),
            pltpu.VMEM((1, funcs), jnp.int32),
            pltpu.VMEM((1, funcs), F32),
            pltpu.VMEM(box, F32),
            pltpu.VMEM(box, F32),
            pltpu.VMEM(box, BF16),
            pltpu.VMEM(box, F32),
            pltpu.VMEM((chunks, plane, 2 * funcs), BF16),
            pltpu.VMEM((chunks, plane, 2 * funcs), BF16),
            pltpu.VMEM((10, plane, plane), BF16),
            pltpu.SMEM((3 * side,), F32),
            pltpu.VMEM((chunks, groups, 2 * cap, plane), BF16),
            pltpu.VMEM((chunks, groups, 2 * cap, plane), BF16),
            pltpu.VMEM((groups * 2 * cap, 2 * funcs), F32),
            pltpu.VMEM((side, plane), F32),
            pltpu.VMEM((side // 2, plane), F32),
            pltpu.VMEM((groups, side // 2, plane), F32),
            pltpu.VMEM((groups, cap, funcs), F32),
            pltpu.VMEM((groups, cap, funcs), F32),
            pltpu.VMEM((groups * cap, funcs), BF16),
            pltpu.VMEM((funcs, padded), BF16),
            pltpu.VMEM((plane, funcs), F32),
            dma((12,)),
            dma((chunks, groups)),
            dma((chunks, groups)),
            dma((groups,)),
            dma((groups,)),
            dma((groups,)),
            dma((groups,)),
            dma,
            dma,
        ],
        compiler_params=pltpu.CompilerParams(
            collective_id=0, has_side_effects=True, vmem_limit_bytes=63 * 2**20
        ),
    )(
        magic_taps, kinetic_taps, owners.reshape(1, funcs), kernel_diag.reshape(1, funcs),
        support, potential,
    )
    return (margin, density)


def body(doms, support, potential, magic_taps, kinetic_taps, kernel_diag, owners):
    side = support.shape[0]
    funcs = support.shape[3]
    groups = lax.axis_size("grp")
    cap = max(2, 3 * funcs // (2 * groups))
    fits = side == 16 and magic_taps.shape[0] == 16 and funcs == 128 and groups == 8
    if fits and cap % 8 == 0 and doms > 1:
        return fused_body(doms, support, potential, magic_taps, kinetic_taps, kernel_diag, owners)
    return general_body(support, potential, magic_taps, kinetic_taps, kernel_diag, owners)


def solution(mesh):
    return jax.shard_map(
        functools.partial(body, mesh.shape["dom"]),
        mesh=mesh,
        in_specs=(
            P(None, None, None, ("dom", "grp")),
            P(None, None, None, ("dom", "grp")),
            P(),
            P(),
            P(("dom", "grp")),
            P(("dom", "grp"), None),
        ),
        out_specs=(P(("dom", "grp"), None), P("dom", None)),
        check_vma=False,
    )
```
